1024 devices in a mesh: outer: 4 (over y), tensor: 64 (over z, core), rep: 4 (over x).
Axes of the slice: x: 4, y: 4, z: 32, core: 2. Of those that a mesh axis runs over, the one named last changes fastest.
Arguments:
- master: float32 [64, 112, 128, 128], P('tensor', ('outer', 'rep')), may hold values from -80 to 80
- synced: bfloat16 [64, 112, 128, 128], P('tensor', ('outer', 'rep')), may hold values from -6 to 6
- keep_mask: int32 [64, 112], P('tensor', ('outer', 'rep')), may hold values from 0 to 1, as said below
- resident: bfloat16 [2, 8192, 7168], P(None, 'tensor'), may hold values from -6 to 6
Outputs:
- updated: bfloat16 [2, 8192, 7168], P(None, 'tensor')
The draws below stay inside these ranges and needn't reach their ends.
Inputs may be any that keep to these rules, and one draw needn't show every extreme that they name: `keep_mask`: within one learner shard's block of 7 tiles of one head (aligned blocks along the second dimension) at most 4 are listed, and some block lists exactly 4.
All inputs are finite; a program needn't handle non-finite values.
Results may differ from the reference program's by a relative error of at most 0.0025.
Values may be sent and summed in bfloat16 or wider, within the bound.
No kernel may reach another device: no remote copies, remote signals or barrier semaphores. Data moves between devices by JAX's collectives and lax.ppermute only.
A program may use at most 64 MiB of HBM per device.

```python
import math
import jax
import jax.numpy as jnp

DM = 7168
HEAD_DIM = 128
TILE = 128
HEADS_DEV = 1
LAYERS = 2
KEEP_MOST = 4
HEADS = 64
TPH = 112
TILE_DEV = 7
TILES = 7168
N_OUTER = 4
N_TENSOR = 64
N_REP = 4


def shared_values(key):
    values = jax.random.normal(key, (HEADS, TPH, TILE, TILE), jnp.float32)
    return jnp.clip(values, -6.0, 6.0)


def tile_scales(scale_key, exponent):
    devices_count = N_OUTER * N_TENSOR * N_REP
    head_index = jnp.arange(HEADS)[:, None]
    tile_index = jnp.arange(TPH)[None, :]
    learner_group = tile_index // TILE_DEV
    outer_index = learner_group // N_REP
    rep_index = learner_group % N_REP
    tensor_index = head_index // HEADS_DEV
    position = (outer_index * N_TENSOR + tensor_index) * N_REP + rep_index
    fraction = position.astype(jnp.float32) / max(devices_count - 1, 1)
    spread = jax.random.uniform(scale_key, (HEADS, TPH), jnp.float32, 0.0, 1.0)
    return 0.5 * jnp.power(3.0, exponent * fraction) * jnp.power(3.0, spread)


def draw_synced(key, part):
    shared = shared_values(key)
    return shared.astype(jnp.bfloat16)


def draw_master(key, part):
    shared = shared_values(key)
    key = jax.random.fold_in(key, 7)
    scale_key, jitter_key, head_key, heavy_key, column_key = jax.random.split(key, 5)
    head_factor = jnp.power(10.0, jax.random.uniform(head_key, (HEADS,), jnp.float32, 0.0, 1.0))
    heavy_head = jax.random.randint(heavy_key, (), 0, HEADS)
    head_factor = jnp.where(jnp.arange(HEADS) == heavy_head, 10.0, head_factor)
    column_factor = jnp.power(2.0, jax.random.uniform(column_key, (TILE,), jnp.float32, 0.0, 1.0))
    scales = tile_scales(scale_key, 0.5)
    jitter = jnp.clip(jax.random.normal(jitter_key, (HEADS, TPH, TILE, TILE), jnp.float32), -4.0, 4.0)
    scales = scales * head_factor[:, None]
    moved = shared + scales[:, :, None, None] * column_factor[None, None, None, :] * jitter
    return jnp.clip(moved, -80.0, 80.0)


def draw_keep_mask(key, part):
    key = jax.random.fold_in(key, 11)
    count_key, heavy_key, forced_key, score_key = jax.random.split(key, 4)
    groups = HEADS * N_OUTER * N_REP
    light_counts = jax.random.randint(count_key, (groups,), 0, 3)
    heavy = jax.random.randint(heavy_key, (groups,), 0, 8) == 0
    listed_counts = jnp.where(heavy, KEEP_MOST, light_counts)
    forced = jax.random.randint(forced_key, (), 0, groups)
    listed_counts = jnp.where(jnp.arange(groups) == forced, KEEP_MOST, listed_counts)
    scores = jax.random.randint(score_key, (groups, TILE_DEV), 0, 1 << 20) * TILE_DEV + jnp.arange(TILE_DEV)[None, :]
    ranking = jnp.argsort(jnp.argsort(scores, axis=1), axis=1)
    chosen = (ranking < listed_counts[:, None]).astype(jnp.int32)
    return chosen.reshape(HEADS, N_OUTER * N_REP * TILE_DEV)


def levels(stream_key, dims, cuts, low, largest):
    loudness = 1.0
    for dim, blocks in cuts:
        steps = jax.random.uniform(jax.random.fold_in(jax.random.fold_in(stream_key, 6), dim), (blocks,), jnp.float32, low / len(cuts), largest / len(cuts))
        loudness = loudness * jnp.repeat(jnp.exp(steps), dims[dim] // blocks).reshape((-1,) + (1,) * (len(dims) - 1 - dim))
    return loudness


def scatter_about(stream_key, shape, deviation, most, cuts=(), held_as=jnp.bfloat16):
    result = jax.random.normal(stream_key, shape, jnp.float32) * deviation
    if len(cuts) > 0:
        result = levels(stream_key, shape, cuts, -0.22, 0.18) * result
    return jnp.clip(result, min=-most, max=most).astype(held_as)


def setup_inputs(seed: int = 0) -> dict:
    splits = jax.random.split(jax.random.key(seed), 5)
    return {
        "master": draw_master(jax.random.fold_in(splits[4], 71), 0),
        "synced": draw_synced(jax.random.fold_in(splits[4], 71), 0),
        "keep_mask": draw_keep_mask(jax.random.fold_in(splits[4], 71), 0),
        "resident": scatter_about(splits[3], (LAYERS, HEADS * HEAD_DIM, DM), 1.0, 6.0, ((1, 64),)),
    }


def reference(master, synced, keep_mask, resident):
    difference = (master - synced.astype(jnp.float32)).astype(jnp.bfloat16)
    listed_delta = difference * keep_mask.astype(jnp.bfloat16)[:, :, None, None]
    widened = listed_delta.astype(jnp.float32)
    total = jnp.sum(widened * widened)
    limit = 0.25 * TILE * math.sqrt(TILES)
    factor = jnp.minimum(jnp.float32(1.0), limit / jnp.sqrt(total))
    arranged = widened.reshape(HEADS, LAYERS, HEAD_DIM // TILE, DM // TILE, TILE, TILE)
    arranged = arranged.transpose(1, 0, 2, 4, 3, 5).reshape(LAYERS, HEADS * HEAD_DIM, DM)
    return (resident.astype(jnp.float32) + factor * arranged).astype(jnp.bfloat16)
```

```python
import functools
import math

import jax
import jax.numpy as jnp
from jax import lax
from jax.experimental import pallas as pl
from jax.experimental.pallas import tpu as pltpu
from jax.sharding import Mesh, PartitionSpec as P

SLOTS = 4
TILE = 128


def pick_kernel(mask_ref, master_ref, synced_ref, tiles_ref, note_ref):
    count = mask_ref.shape[1]
    lane = lax.broadcasted_iota(jnp.int32, note_ref.shape[1:], 1)
    note = jnp.zeros(note_ref.shape[1:], jnp.float32)
    where = [jnp.int32(0)] * SLOTS
    used = jnp.int32(0)
    for i in range(count):
        listed = mask_ref[0, i] > 0
        for s in range(SLOTS):
            where[s] = jnp.where(listed & (used == s), i, where[s])
        slot = jnp.where(listed, used, -1)
        note = jnp.where(lane == 1 + i, slot.astype(jnp.float32), note)
        used = used + listed.astype(jnp.int32)
    squares = jnp.zeros((8, TILE), jnp.float32)
    for s in range(SLOTS):
        delta = (master_ref[0, where[s]] - synced_ref[0, where[s]].astype(jnp.float32)).astype(jnp.bfloat16)
        tiles_ref[s] = delta
        wide = jnp.where(used > s, delta.astype(jnp.float32), 0.0)
        squares = squares + jnp.sum((wide * wide).reshape(-1, 8, TILE), axis=0)
    note = jnp.where(lane == 0, jnp.sum(squares), note)
    note_ref[...] = jnp.broadcast_to(note[None], note_ref.shape)


def plane_kernel(outers, reps, notes_ref, sums_ref, table_ref):
    core = lax.axis_index("core")
    rows = notes_ref[:, 0, :]
    lane = lax.broadcasted_iota(jnp.int32, rows.shape, 1)
    total = jnp.sum(jnp.where(lane == 0, rows, 0.0))
    sums_ref[...] = jnp.full(sums_ref.shape, total, jnp.float32)
    for y in range(outers):
        mine = notes_ref[pl.ds((y * 2 + core) * reps, reps), 0, :]
        table_ref[y * reps:(y + 1) * reps, :] = mine.astype(jnp.int32)


def apply_kernel(limit, count, table_ref, sums_ref, tiles_ref, resident_ref, out_ref):
    shard = pl.program_id(0)
    total = jnp.sum(sums_ref[:, 0:1, :], axis=0)
    factor = jnp.minimum(jnp.float32(1.0), limit / jnp.sqrt(total))
    out_ref[...] = resident_ref[...]
    for i in range(count):
        slot = table_ref[shard, 1 + i]

        @pl.when(slot >= 0)
        def _():
            cols = slice(i * TILE, (i + 1) * TILE)
            moved = factor * tiles_ref[slot].astype(jnp.float32)
            out_ref[0, :, cols] = (resident_ref[0, :, cols].astype(jnp.float32) + moved).astype(jnp.bfloat16)


def body(master, synced, keep_mask, resident):
    outers, chips, cores, reps = (lax.axis_size(a) for a in ("outer", "z", "core", "rep"))
    _, count, side, _ = master.shape
    layers, rows, width = resident.shape
    shards = outers * reps
    plane = shards * cores
    vmem = pl.BlockSpec(memory_space=pltpu.VMEM)
    smem = pl.BlockSpec(memory_space=pltpu.SMEM)
    with jax.named_scope("pick"):
        tiles, notes = pl.pallas_call(
            pick_kernel,
            out_shape=(
                jax.ShapeDtypeStruct((SLOTS, side, side), jnp.bfloat16),
                jax.ShapeDtypeStruct((plane, 8, TILE), jnp.float32),
            ),
            in_specs=[smem, vmem, vmem],
            out_specs=(vmem, vmem),
        )(keep_mask, master, synced)
    with jax.named_scope("gather"):
        gathered = lax.all_gather(tiles, ("outer", "rep"), axis=0, tiled=True)
    with jax.named_scope("plane_sum"):
        notes = lax.all_to_all(notes, ("outer", "core", "rep"), 0, 0, tiled=True)
        sums, table = pl.pallas_call(
            functools.partial(plane_kernel, outers, reps),
            out_shape=(
                jax.ShapeDtypeStruct((chips, 8, TILE), jnp.float32),
                jax.ShapeDtypeStruct((shards, TILE), jnp.int32),
            ),
            in_specs=[vmem],
            out_specs=(vmem, vmem),
        )(notes)
    with jax.named_scope("z_sum"):
        sums = lax.all_to_all(sums, "z", 0, 0, tiled=True)
    limit = 0.25 * side * math.sqrt(count * plane * chips)
    per_layer = width // (count * side)
    place = pl.BlockSpec((1, rows, count * side), lambda j, t: (j // per_layer, 0, j % per_layer))
    with jax.named_scope("apply"):
        return pl.pallas_call(
            functools.partial(apply_kernel, limit, count),
            out_shape=jax.ShapeDtypeStruct(resident.shape, resident.dtype),
            grid_spec=pltpu.PrefetchScalarGridSpec(
                num_scalar_prefetch=1,
                grid=(shards,),
                in_specs=[
                    pl.BlockSpec((chips, 8, TILE), lambda j, t: (0, 0, 0)),
                    pl.BlockSpec((SLOTS, side, side), lambda j, t: (j, 0, 0)),
                    place,
                ],
                out_specs=place,
            ),
        )(table, sums, gathered, resident)


def solution(mesh):
    outers, tensors, reps = mesh.devices.shape
    fine = Mesh(mesh.devices.reshape(outers, tensors // 2, 2, reps), ("outer", "z", "core", "rep"))
    head = ("z", "core")
    placed = (
        P(head, ("outer", "rep"), None, None),
        P(head, ("outer", "rep"), None, None),
        P(head, ("outer", "rep")),
        P(None, head, None),
    )
    return jax.shard_map(
        body, mesh=fine, in_specs=placed, out_specs=P(None, head, None), check_vma=False
    )
```

```python
import functools
import math

import jax
import jax.numpy as jnp
from jax import lax
from jax.experimental import pallas as pl
from jax.experimental.pallas import tpu as pltpu
from jax.sharding import Mesh, PartitionSpec as P

SLOTS = 4
TILE = 128
PARTS = 8
ROOM = 12 * 2**20
ALL = ("outer", "z", "core", "rep")
PLANE = ("outer", "core", "rep")


def pick_kernel(mask_ref, master_ref, synced_ref, tiles_ref, note_ref):
    count = mask_ref.shape[1]
    where = [jnp.int32(0)] * SLOTS
    used = jnp.int32(0)
    for i in range(count):
        listed = mask_ref[0, i] > 0
        for s in range(SLOTS):
            where[s] = jnp.where(listed & (used == s), i, where[s])
        used = used + listed.astype(jnp.int32)
    squares = jnp.zeros((8, TILE), jnp.float32)
    for s in range(SLOTS):
        delta = (master_ref[0, where[s]] - synced_ref[0, where[s]].astype(jnp.float32)).astype(jnp.bfloat16)
        tiles_ref[s] = delta
        wide = jnp.where(used > s, delta.astype(jnp.float32), 0.0)
        squares = squares + jnp.sum((wide * wide).reshape(-1, 8, TILE), axis=0)
    lane = lax.broadcasted_iota(jnp.int32, note_ref.shape[1:], 1)
    note = jnp.where(lane == 0, jnp.sum(squares), 0.0)
    for k, entry in enumerate([used] + where):
        note = jnp.where(lane == 1 + k, entry.astype(jnp.float32), note)
    note_ref[...] = jnp.broadcast_to(note[None], note_ref.shape)


def plane_kernel(outers, reps, notes_ref, sum_ref, table_ref):
    core = lax.axis_index("core")
    total = jnp.sum(notes_ref[...], axis=0)
    sum_ref[...] = jnp.broadcast_to(total[:, 0:1], total.shape)
    lane = lax.broadcasted_iota(jnp.int32, (reps, TILE), 1)
    for y in range(outers):
        mine = notes_ref[pl.ds((y * 2 + core) * reps, reps), 0, :]
        table_ref[y * reps:(y + 1) * reps, :] = jnp.where(lane == 0, 0.0, mine).astype(jnp.int32)


def each_listed(table_ref, act):
    shards = table_ref.shape[0]
    tile_count = 7

    def over_shards(j, _):
        def over_slots(s, _):
            act(j * SLOTS + s, j * tile_count + table_ref[j, 2 + s])
            return 0

        return lax.fori_loop(0, table_ref[j, 1], over_slots, 0)

    lax.fori_loop(0, shards, over_shards, 0)


def tile_of(ref, tile):
    layers, rows, width = ref.shape
    per_layer = width // TILE
    layer = tile // per_layer
    start = pl.multiple_of((tile - layer * per_layer) * TILE, TILE)
    return ref.at[layer, :, pl.ds(start, TILE)]


def base_kernel(table_ref, resident_ref, base_ref, stage_ref, whole_sem, tile_sem):
    layers, rows, _ = resident_ref.shape
    chunk = rows // PARTS
    copies = [
        pltpu.make_async_copy(
            resident_ref.at[l, pl.ds(k * chunk, chunk)], base_ref.at[l, pl.ds(k * chunk, chunk)], whole_sem.at[l, k]
        )
        for l in range(layers)
        for k in range(PARTS)
    ]

    def staged(slot, tile):
        return pltpu.make_async_copy(tile_of(resident_ref, tile), stage_ref.at[slot], tile_sem.at[slot])

    each_listed(table_ref, lambda slot, tile: staged(slot, tile).start())
    for copy in copies:
        copy.start()
    each_listed(table_ref, lambda slot, tile: staged(slot, tile).wait())
    for copy in copies:
        copy.wait()


def apply_kernel(limit, table_ref, sums_ref, stage_ref, tiles_ref, base_ref, out_ref, new_ref, sem):
    del base_ref
    total = jnp.sum(sums_ref[...], axis=0)
    factor = jnp.minimum(jnp.float32(1.0), limit / jnp.sqrt(total))

    def written(slot, tile):
        return pltpu.make_async_copy(new_ref.at[slot], tile_of(out_ref, tile), sem.at[slot])

    def update(slot, tile):
        moved = factor[None] * tiles_ref[slot].astype(jnp.float32).reshape(-1, 8, TILE)
        new_ref[slot] = (stage_ref[slot].astype(jnp.float32) + moved.reshape(TILE, TILE)).astype(jnp.bfloat16)
        written(slot, tile).start()

    each_listed(table_ref, update)
    each_listed(table_ref, lambda slot, tile: written(slot, tile).wait())


def body(master, synced, keep_mask, resident):
    outers, chips, cores, reps = (lax.axis_size(a) for a in ALL)
    _, count, side, _ = master.shape
    shards = outers * reps
    plane = shards * cores
    vmem = pl.BlockSpec(memory_space=pltpu.VMEM)
    smem = pl.BlockSpec(memory_space=pltpu.SMEM)
    hbm = pl.BlockSpec(memory_space=pltpu.HBM)
    params = pltpu.CompilerParams(vmem_limit_bytes=ROOM)
    with jax.named_scope("pick"):
        tiles, notes = pl.pallas_call(
            pick_kernel,
            out_shape=(
                jax.ShapeDtypeStruct((SLOTS, side, side), jnp.bfloat16),
                jax.ShapeDtypeStruct((plane, 8, TILE), jnp.float32),
            ),
            in_specs=[smem, vmem, vmem],
            out_specs=(vmem, vmem),
            compiler_params=params,
        )(keep_mask, master, synced)
    with jax.named_scope("plane_sum"):
        notes = lax.all_to_all(notes, PLANE, 0, 0, tiled=True)
        plane_total, table = pl.pallas_call(
            functools.partial(plane_kernel, outers, reps),
            out_shape=(
                jax.ShapeDtypeStruct((8, TILE), jnp.float32),
                jax.ShapeDtypeStruct((shards, TILE), jnp.int32),
            ),
            in_specs=[vmem],
            out_specs=(vmem, vmem),
            compiler_params=params,
        )(notes)
    tiles, plane_total = lax.optimization_barrier((tiles, plane_total))
    with jax.named_scope("gather"):
        spread = jnp.broadcast_to(tiles[None], (shards,) + tiles.shape)
        gathered = lax.all_to_all(spread, ("outer", "rep"), 0, 0, tiled=True)
        gathered = gathered.reshape(shards * SLOTS, side, side)
    with jax.named_scope("z_shift"):
        pairs = []
        for o in range(outers):
            for z in range(chips):
                for c in range(cores):
                    for r in range(reps):
                        there = (z + (o * cores + c) * reps + r - plane // 2 + 1) % chips
                        pairs.append(
                            (((o * chips + z) * cores + c) * reps + r, ((o * chips + there) * cores + c) * reps + r)
                        )
        other = lax.ppermute(plane_total, ALL, pairs)
    with jax.named_scope("base"):
        base, stage = pl.pallas_call(
            base_kernel,
            out_shape=(
                jax.ShapeDtypeStruct(resident.shape, resident.dtype),
                jax.ShapeDtypeStruct((shards * SLOTS, side, side), resident.dtype),
            ),
            in_specs=[smem, hbm],
            out_specs=(hbm, vmem),
            scratch_shapes=[
                pltpu.SemaphoreType.DMA((resident.shape[0], PARTS)),
                pltpu.SemaphoreType.DMA((shards * SLOTS,)),
            ],
            compiler_params=params,
            cost_estimate=pl.CostEstimate(flops=0, bytes_accessed=4 * resident.size, transcendentals=0),
        )(table, resident)
    other, gathered, base = lax.optimization_barrier((other, gathered, base))
    with jax.named_scope("z_sum"):
        sums = lax.all_to_all(jnp.broadcast_to(other[None], (plane, 8, TILE)), PLANE, 0, 0, tiled=True)
    limit = 0.25 * side * math.sqrt(count * plane * chips)
    limit = limit * math.sqrt(plane / chips)
    with jax.named_scope("apply"):
        return pl.pallas_call(
            functools.partial(apply_kernel, limit),
            out_shape=jax.ShapeDtypeStruct(resident.shape, resident.dtype),
            in_specs=[smem, vmem, vmem, vmem, hbm],
            out_specs=hbm,
            scratch_shapes=[
                pltpu.VMEM((shards * SLOTS, side, side), jnp.bfloat16),
                pltpu.SemaphoreType.DMA((shards * SLOTS,)),
            ],
            input_output_aliases={4: 0},
            compiler_params=params,
        )(table, sums, stage, gathered, base)


def solution(mesh):
    outers, tensors, reps = mesh.devices.shape
    fine = Mesh(mesh.devices.reshape(outers, tensors // 2, 2, reps), ALL)
    head = ("z", "core")
    placed = (
        P(head, ("outer", "rep"), None, None),
        P(head, ("outer", "rep"), None, None),
        P(head, ("outer", "rep")),
        P(None, head, None),
    )
    return jax.shard_map(
        body, mesh=fine, in_specs=placed, out_specs=P(None, head, None), check_vma=False
    )
```

```python
import functools
import math

import jax
import jax.numpy as jnp
from jax import lax
from jax.experimental import pallas as pl
from jax.experimental.pallas import tpu as pltpu
from jax.sharding import Mesh, PartitionSpec as P

SLOTS = 4
TILE = 128
SMALL = 4 * 2**20
LARGE = 53 * 10**6
ALL = ("outer", "z", "core", "rep")
PLANE = ("outer", "core", "rep")
PEERS = ("outer", "rep")


def pick_kernel(mask_hbm, master_hbm, synced_hbm, spread_hbm, note_ref, mask_ref, master_ref, synced_ref, tiles_ref, sem, out_sem):
    loads = [
        pltpu.make_async_copy(mask_hbm, mask_ref, sem.at[0]),
        pltpu.make_async_copy(master_hbm, master_ref, sem.at[1]),
        pltpu.make_async_copy(synced_hbm, synced_ref, sem.at[2]),
    ]
    for load in loads:
        load.start()
    loads[0].wait()
    where = [jnp.int32(0)] * SLOTS
    used = jnp.int32(0)
    for i in range(mask_ref.shape[1]):
        listed = mask_ref[0, i] > 0
        for s in range(SLOTS):
            where[s] = jnp.where(listed & (used == s), i, where[s])
        used = used + listed.astype(jnp.int32)
    for load in loads[1:]:
        load.wait()
    squares = jnp.zeros((8, TILE), jnp.float32)
    for s in range(SLOTS):
        delta = (master_ref[0, where[s]] - synced_ref[0, where[s]].astype(jnp.float32)).astype(jnp.bfloat16)
        tiles_ref[s] = delta
        wide = jnp.where(used > s, delta.astype(jnp.float32), 0.0)
        squares = squares + jnp.sum((wide * wide).reshape(-1, 8, TILE), axis=0)
    sends = [
        pltpu.make_async_copy(tiles_ref, spread_hbm.at[j], out_sem.at[j]) for j in range(spread_hbm.shape[0])
    ]
    for send in sends:
        send.start()
    lane = lax.broadcasted_iota(jnp.int32, note_ref.shape, 1)
    note = jnp.where(lane == 0, jnp.sum(squares), 0.0)
    for k, entry in enumerate([used] + where):
        note = jnp.where(lane == 1 + k, entry.astype(jnp.float32), note)
    note_ref[...] = note
    for send in sends:
        send.wait()


def column_kernel(column_ref, note_ref, notes_ref):
    total = jnp.sum(column_ref[...], axis=0, keepdims=True)
    note = note_ref[...]
    lane = lax.broadcasted_iota(jnp.int32, note.shape, 1)
    note = jnp.where(lane == 0, total, note)
    notes_ref[...] = jnp.broadcast_to(note[None], notes_ref.shape)


def plane_kernel(limit, outers, reps, notes_ref, factor_ref, table_ref):
    core = lax.axis_index("core")
    total = jnp.sum(notes_ref[...], axis=0)
    total = jnp.broadcast_to(total[:, 0:1], total.shape)
    factor_ref[...] = jnp.minimum(jnp.float32(1.0), limit / jnp.sqrt(total))
    lane = lax.broadcasted_iota(jnp.int32, (reps, TILE), 1)
    for y in range(outers):
        mine = notes_ref[pl.ds((y * 2 + core) * reps, reps), 0, :]
        table_ref[y * reps:(y + 1) * reps, :] = jnp.where(lane == 0, 0.0, mine).astype(jnp.int32)


def apply_kernel(count, table_ref, factor_ref, tiles_ref, resident_hbm, out_hbm, rows_ref, in_sem, out_sem):
    shards = table_ref.shape[0]
    wide = count * TILE
    per_layer = resident_hbm.shape[2] // wide

    def block(ref, j):
        return ref.at[j // per_layer, :, pl.ds((j % per_layer) * wide, wide)]

    loads = [pltpu.make_async_copy(block(resident_hbm, j), block(rows_ref, j), in_sem.at[j]) for j in range(shards)]
    stores = [pltpu.make_async_copy(block(rows_ref, j), block(out_hbm, j), out_sem.at[j]) for j in range(shards)]
    for load in loads:
        load.start()
    factor = factor_ref[...][None]
    for j in range(shards):
        loads[j].wait()

        def update(s, _):
            start = pl.multiple_of((j % per_layer) * wide + table_ref[j, 2 + s] * TILE, TILE)
            place = (j // per_layer, slice(None), pl.ds(start, TILE))
            moved = (factor * tiles_ref[j * SLOTS + s].astype(jnp.float32).reshape(-1, 8, TILE)).reshape(TILE, TILE)
            rows_ref[place] = (rows_ref[place].astype(jnp.float32) + moved).astype(jnp.bfloat16)
            return 0

        lax.fori_loop(0, table_ref[j, 1], update, 0)
        stores[j].start()
    for store in stores:
        store.wait()


def body(master, synced, keep_mask, resident):
    outers, chips, cores, reps = (lax.axis_size(a) for a in ALL)
    _, count, side, _ = master.shape
    shards = outers * reps
    plane = shards * cores
    limit = 0.25 * side * math.sqrt(count * plane * chips)
    vmem = pl.BlockSpec(memory_space=pltpu.VMEM)
    smem = pl.BlockSpec(memory_space=pltpu.SMEM)
    hbm = pl.BlockSpec(memory_space=pl.ANY)
    small = pltpu.CompilerParams(vmem_limit_bytes=SMALL)
    large = pltpu.CompilerParams(vmem_limit_bytes=LARGE)
    with jax.named_scope("pick"):
        spread, note = pl.pallas_call(
            pick_kernel,
            out_shape=(
                jax.ShapeDtypeStruct((shards, SLOTS, side, side), jnp.bfloat16),
                jax.ShapeDtypeStruct((8, TILE), jnp.float32),
            ),
            in_specs=[hbm, hbm, hbm],
            out_specs=(hbm, vmem),
            scratch_shapes=[
                pltpu.SMEM(keep_mask.shape, keep_mask.dtype),
                pltpu.VMEM(master.shape, master.dtype),
                pltpu.VMEM(synced.shape, synced.dtype),
                pltpu.VMEM((SLOTS, side, side), jnp.bfloat16),
                pltpu.SemaphoreType.DMA((3,)),
                pltpu.SemaphoreType.DMA((shards,)),
            ],
        )(keep_mask, master, synced)
    with jax.named_scope("gather"):
        gathered = lax.all_to_all(spread, PEERS, 0, 0, tiled=True)
        gathered = gathered.reshape(shards * SLOTS, side, side)
    with jax.named_scope("z_sum"):
        column = lax.all_gather(note[:1], "z", axis=0, tiled=True)
        notes = pl.pallas_call(
            column_kernel,
            out_shape=jax.ShapeDtypeStruct((plane, 8, TILE), jnp.float32),
            in_specs=[vmem, vmem],
            out_specs=vmem,
            compiler_params=small,
        )(column, note)
    notes, gathered = lax.optimization_barrier((notes, gathered))
    with jax.named_scope("plane_sum"):
        notes = lax.all_to_all(notes, PLANE, 0, 0, tiled=True)
        factor, table = pl.pallas_call(
            functools.partial(plane_kernel, limit, outers, reps),
            out_shape=(
                jax.ShapeDtypeStruct((8, TILE), jnp.float32),
                jax.ShapeDtypeStruct((shards, TILE), jnp.int32),
            ),
            in_specs=[vmem],
            out_specs=(vmem, vmem),
            compiler_params=small,
        )(notes)
    with jax.named_scope("apply"):
        return pl.pallas_call(
            functools.partial(apply_kernel, count),
            out_shape=jax.ShapeDtypeStruct(resident.shape, resident.dtype),
            in_specs=[smem, vmem, vmem, hbm],
            out_specs=hbm,
            scratch_shapes=[
                pltpu.VMEM(resident.shape, resident.dtype),
                pltpu.SemaphoreType.DMA((shards,)),
                pltpu.SemaphoreType.DMA((shards,)),
            ],
            compiler_params=large,
        )(table, factor, gathered, resident)


def solution(mesh):
    outers, tensors, reps = mesh.devices.shape
    fine = Mesh(mesh.devices.reshape(outers, tensors // 2, 2, reps), ALL)
    head = ("z", "core")
    placed = (
        P(head, PEERS, None, None),
        P(head, PEERS, None, None),
        P(head, PEERS),
        P(None, head, None),
    )
    return jax.shard_map(
        body, mesh=fine, in_specs=placed, out_specs=P(None, head, None), check_vma=False
    )
```

```python
import functools
import math

import jax
import jax.numpy as jnp
from jax import lax
from jax.experimental import pallas as pl
from jax.experimental.pallas import tpu as pltpu
from jax.sharding import Mesh, PartitionSpec as P

SLOTS = 4
TILE = 128
PARTS = 8
SMALL = 4 * 2**20
LARGE = 53 * 10**6
PICK = 568 * 10**5
ALL = ("outer", "z", "core", "rep")
PLANE = ("outer", "core", "rep")
PEERS = ("outer", "rep")


def pick_kernel(mask_hbm, master_hbm, synced_hbm, spread_hbm, notes_ref, mask_ref, master_ref, synced_ref, tiles_ref, sem, out_sem):
    loads = [
        pltpu.make_async_copy(mask_hbm, mask_ref, sem.at[0]),
        pltpu.make_async_copy(master_hbm, master_ref, sem.at[1]),
        pltpu.make_async_copy(synced_hbm, synced_ref, sem.at[2]),
    ]
    for load in loads:
        load.start()
    loads[0].wait()
    where = [jnp.int32(0)] * SLOTS
    used = jnp.int32(0)
    for i in range(mask_ref.shape[1]):
        listed = mask_ref[0, i] > 0
        for s in range(SLOTS):
            where[s] = jnp.where(listed & (used == s), i, where[s])
        used = used + listed.astype(jnp.int32)
    for load in loads[1:]:
        load.wait()
    squares = jnp.zeros((8, TILE), jnp.float32)
    for s in range(SLOTS):
        delta = (master_ref[0, where[s]] - synced_ref[0, where[s]].astype(jnp.float32)).astype(jnp.bfloat16)
        tiles_ref[s] = delta
        wide = jnp.where(used > s, delta.astype(jnp.float32), 0.0)
        squares = squares + jnp.sum((wide * wide).reshape(-1, 8, TILE), axis=0)
    sends = [
        pltpu.make_async_copy(tiles_ref, spread_hbm.at[j], out_sem.at[j]) for j in range(spread_hbm.shape[0])
    ]
    for send in sends:
        send.start()
    lane = lax.broadcasted_iota(jnp.int32, notes_ref.shape[1:], 1)
    note = jnp.where(lane == 0, jnp.sum(squares), 0.0)
    for k, entry in enumerate([used] + where):
        note = jnp.where(lane == 1 + k, entry.astype(jnp.float32), note)
    notes_ref[...] = jnp.broadcast_to(note[None], notes_ref.shape)
    for send in sends:
        send.wait()


def plane_kernel(outers, reps, notes_ref, sum_ref, table_ref):
    core = lax.axis_index("core")
    total = jnp.sum(notes_ref[...], axis=0)
    sum_ref[...] = jnp.broadcast_to(total[:, 0:1], total.shape)
    lane = lax.broadcasted_iota(jnp.int32, (reps, TILE), 1)
    for y in range(outers):
        mine = notes_ref[pl.ds((y * 2 + core) * reps, reps), 0, :]
        table_ref[y * reps:(y + 1) * reps, :] = jnp.where(lane == 0, 0.0, mine).astype(jnp.int32)


def each_listed(table_ref, act):
    shards = table_ref.shape[0]
    tile_count = 7

    def over_shards(j, _):
        def over_slots(s, _):
            act(j * SLOTS + s, j * tile_count + table_ref[j, 2 + s])
            return 0

        return lax.fori_loop(0, table_ref[j, 1], over_slots, 0)

    lax.fori_loop(0, shards, over_shards, 0)


def tile_of(ref, tile):
    layers, rows, width = ref.shape
    per_layer = width // TILE
    layer = tile // per_layer
    start = pl.multiple_of((tile - layer * per_layer) * TILE, TILE)
    return ref.at[layer, :, pl.ds(start, TILE)]


def base_kernel(resident_ref, base_ref, sem):
    layers, rows, _ = resident_ref.shape
    chunk = rows // PARTS
    copies = [
        pltpu.make_async_copy(
            resident_ref.at[l, pl.ds(k * chunk, chunk)], base_ref.at[l, pl.ds(k * chunk, chunk)], sem.at[l, k]
        )
        for l in range(layers)
        for k in range(PARTS)
    ]
    for copy in copies:
        copy.start()
    for copy in copies:
        copy.wait()


def apply_kernel(limit, table_ref, sums_ref, tiles_ref, resident_ref, base_ref, out_ref, new_ref, in_sem, out_sem):
    del base_ref

    def loaded(slot, tile):
        return pltpu.make_async_copy(tile_of(resident_ref, tile), new_ref.at[slot], in_sem.at[slot])

    def written(slot, tile):
        return pltpu.make_async_copy(new_ref.at[slot], tile_of(out_ref, tile), out_sem.at[slot])

    each_listed(table_ref, lambda slot, tile: loaded(slot, tile).start())
    total = jnp.sum(sums_ref[...], axis=0)
    factor = jnp.minimum(jnp.float32(1.0), limit / jnp.sqrt(total))

    def update(slot, tile):
        loaded(slot, tile).wait()
        moved = factor[None] * tiles_ref[slot].astype(jnp.float32).reshape(-1, 8, TILE)
        new_ref[slot] = (new_ref[slot].astype(jnp.float32) + moved.reshape(TILE, TILE)).astype(jnp.bfloat16)
        written(slot, tile).start()

    each_listed(table_ref, update)
    each_listed(table_ref, lambda slot, tile: written(slot, tile).wait())


def body(master, synced, keep_mask, resident):
    outers, chips, cores, reps = (lax.axis_size(a) for a in ALL)
    _, count, side, _ = master.shape
    shards = outers * reps
    plane = shards * cores
    vmem = pl.BlockSpec(memory_space=pltpu.VMEM)
    smem = pl.BlockSpec(memory_space=pltpu.SMEM)
    hbm = pl.BlockSpec(memory_space=pl.ANY)
    small = pltpu.CompilerParams(vmem_limit_bytes=SMALL)
    large = pltpu.CompilerParams(vmem_limit_bytes=LARGE)
    with jax.named_scope("pick"):
        spread, notes = pl.pallas_call(
            pick_kernel,
            out_shape=(
                jax.ShapeDtypeStruct((shards, SLOTS, side, side), jnp.bfloat16),
                jax.ShapeDtypeStruct((plane, 8, TILE), jnp.float32),
            ),
            in_specs=[hbm, hbm, hbm],
            out_specs=(hbm, vmem),
            scratch_shapes=[
                pltpu.SMEM(keep_mask.shape, keep_mask.dtype),
                pltpu.VMEM(master.shape, master.dtype),
                pltpu.VMEM(synced.shape, synced.dtype),
                pltpu.VMEM((SLOTS, side, side), jnp.bfloat16),
                pltpu.SemaphoreType.DMA((3,)),
                pltpu.SemaphoreType.DMA((shards,)),
            ],
            compiler_params=pltpu.CompilerParams(vmem_limit_bytes=PICK),
        )(keep_mask, master, synced)
    with jax.named_scope("plane_sum"):
        notes = lax.all_to_all(notes, PLANE, 0, 0, tiled=True)
        plane_total, table = pl.pallas_call(
            functools.partial(plane_kernel, outers, reps),
            out_shape=(
                jax.ShapeDtypeStruct((8, TILE), jnp.float32),
                jax.ShapeDtypeStruct((shards, TILE), jnp.int32),
            ),
            in_specs=[vmem],
            out_specs=(vmem, vmem),
            compiler_params=small,
        )(notes)
    spread, plane_total = lax.optimization_barrier((spread, plane_total))
    with jax.named_scope("gather"):
        gathered = lax.all_to_all(spread, PEERS, 0, 0, tiled=True)
        gathered = gathered.reshape(shards * SLOTS, side, side)
    with jax.named_scope("z_shift"):
        pairs = []
        for o in range(outers):
            for z in range(chips):
                for c in range(cores):
                    for r in range(reps):
                        there = (z + (o * cores + c) * reps + r - plane // 2 + 1) % chips
                        pairs.append(
                            (((o * chips + z) * cores + c) * reps + r, ((o * chips + there) * cores + c) * reps + r)
                        )
        other = lax.ppermute(plane_total, ALL, pairs)
    with jax.named_scope("base"):
        base = pl.pallas_call(
            base_kernel,
            out_shape=jax.ShapeDtypeStruct(resident.shape, resident.dtype),
            in_specs=[hbm],
            out_specs=hbm,
            scratch_shapes=[pltpu.SemaphoreType.DMA((resident.shape[0], PARTS))],
            compiler_params=large,
            cost_estimate=pl.CostEstimate(flops=0, bytes_accessed=4 * resident.size, transcendentals=0),
        )(resident)
    other, gathered, base = lax.optimization_barrier((other, gathered, base))
    with jax.named_scope("z_sum"):
        sums = lax.all_to_all(jnp.broadcast_to(other[None], (plane, 8, TILE)), PLANE, 0, 0, tiled=True)
    limit = 0.25 * side * math.sqrt(count * plane * chips)
    limit = limit * math.sqrt(plane / chips)
    with jax.named_scope("apply"):
        return pl.pallas_call(
            functools.partial(apply_kernel, limit),
            out_shape=jax.ShapeDtypeStruct(resident.shape, resident.dtype),
            in_specs=[smem, vmem, vmem, hbm, hbm],
            out_specs=hbm,
            scratch_shapes=[
                pltpu.VMEM((shards * SLOTS, side, side), jnp.bfloat16),
                pltpu.SemaphoreType.DMA((shards * SLOTS,)),
                pltpu.SemaphoreType.DMA((shards * SLOTS,)),
            ],
            input_output_aliases={4: 0},
            compiler_params=large,
        )(table, sums, gathered, resident, base)


def solution(mesh):
    outers, tensors, reps = mesh.devices.shape
    fine = Mesh(mesh.devices.reshape(outers, tensors // 2, 2, reps), ALL)
    head = ("z", "core")
    placed = (
        P(head, PEERS, None, None),
        P(head, PEERS, None, None),
        P(head, PEERS),
        P(None, head, None),
    )
    return jax.shard_map(
        body, mesh=fine, in_specs=placed, out_specs=P(None, head, None), check_vma=False
    )
```

```python
import functools
import math

import jax
import jax.numpy as jnp
from jax import lax
from jax.experimental import pallas as pl
from jax.experimental.pallas import tpu as pltpu
from jax.sharding import Mesh, PartitionSpec as P

SLOTS = 4
TILE = 128
SMALL = 4 * 2**20
LARGE = 53 * 10**6
ALL = ("outer", "z", "core", "rep")
PLANE = ("outer", "core", "rep")
ROW = ("core", "rep")
PEERS = ("outer", "rep")


def pick_kernel(mask_hbm, master_hbm, synced_hbm, spread_hbm, note_ref, mask_ref, master_ref, synced_ref, tiles_ref, sem, out_sem):
    loads = [
        pltpu.make_async_copy(mask_hbm, mask_ref, sem.at[0]),
        pltpu.make_async_copy(master_hbm, master_ref, sem.at[1]),
        pltpu.make_async_copy(synced_hbm, synced_ref, sem.at[2]),
    ]
    for load in loads:
        load.start()
    loads[0].wait()
    where = [jnp.int32(0)] * SLOTS
    used = jnp.int32(0)
    for i in range(mask_ref.shape[1]):
        listed = mask_ref[0, i] > 0
        for s in range(SLOTS):
            where[s] = jnp.where(listed & (used == s), i, where[s])
        used = used + listed.astype(jnp.int32)
    for load in loads[1:]:
        load.wait()
    squares = jnp.zeros((8, TILE), jnp.float32)
    for s in range(SLOTS):
        delta = (master_ref[0, where[s]] - synced_ref[0, where[s]].astype(jnp.float32)).astype(jnp.bfloat16)
        tiles_ref[s] = delta
        wide = jnp.where(used > s, delta.astype(jnp.float32), 0.0)
        squares = squares + jnp.sum((wide * wide).reshape(-1, 8, TILE), axis=0)
    sends = [
        pltpu.make_async_copy(tiles_ref, spread_hbm.at[j], out_sem.at[j]) for j in range(spread_hbm.shape[0])
    ]
    for send in sends:
        send.start()
    lane = lax.broadcasted_iota(jnp.int32, note_ref.shape[1:], 1)
    note = jnp.where(lane == 0, jnp.sum(squares), 0.0)
    for k, entry in enumerate([used] + where):
        note = jnp.where(lane == 1 + k, entry.astype(jnp.float32), note)
    note_ref[...] = jnp.broadcast_to(note[None], note_ref.shape)
    for send in sends:
        send.wait()


def row_kernel(notes_ref, sum_ref):
    total = jnp.sum(notes_ref[...], axis=0)
    sum_ref[...] = jnp.broadcast_to(total[:, 0:1], total.shape)


def mix_kernel(other_ref, note_ref, notes_ref):
    note = note_ref[0]
    lane = lax.broadcasted_iota(jnp.int32, note.shape, 1)
    note = jnp.where(lane == 0, other_ref[...], note)
    notes_ref[...] = jnp.broadcast_to(note[None], notes_ref.shape)


def plane_kernel(limit, outers, reps, notes_ref, factor_ref, table_ref):
    core = lax.axis_index("core")
    total = jnp.sum(notes_ref[...], axis=0)
    total = jnp.broadcast_to(total[:, 0:1], total.shape)
    factor_ref[...] = jnp.minimum(jnp.float32(1.0), limit / jnp.sqrt(total))
    lane = lax.broadcasted_iota(jnp.int32, (reps, TILE), 1)
    for y in range(outers):
        mine = notes_ref[pl.ds((y * 2 + core) * reps, reps), 0, :]
        table_ref[y * reps:(y + 1) * reps, :] = jnp.where(lane == 0, 0.0, mine).astype(jnp.int32)


def apply_kernel(count, table_ref, factor_ref, tiles_ref, resident_hbm, out_hbm, rows_ref, in_sem, out_sem):
    shards = table_ref.shape[0]
    wide = count * TILE
    per_layer = resident_hbm.shape[2] // wide

    def block(ref, j):
        return ref.at[j // per_layer, :, pl.ds((j % per_layer) * wide, wide)]

    loads = [pltpu.make_async_copy(block(resident_hbm, j), block(rows_ref, j), in_sem.at[j]) for j in range(shards)]
    stores = [pltpu.make_async_copy(block(rows_ref, j), block(out_hbm, j), out_sem.at[j]) for j in range(shards)]
    for load in loads:
        load.start()
    factor = factor_ref[...][None]
    for j in range(shards):
        loads[j].wait()

        def update(s, _):
            start = pl.multiple_of((j % per_layer) * wide + table_ref[j, 2 + s] * TILE, TILE)
            place = (j // per_layer, slice(None), pl.ds(start, TILE))
            moved = (factor * tiles_ref[j * SLOTS + s].astype(jnp.float32).reshape(-1, 8, TILE)).reshape(TILE, TILE)
            rows_ref[place] = (rows_ref[place].astype(jnp.float32) + moved).astype(jnp.bfloat16)
            return 0

        lax.fori_loop(0, table_ref[j, 1], update, 0)
        stores[j].start()
    for store in stores:
        store.wait()


def body(master, synced, keep_mask, resident):
    outers, chips, cores, reps = (lax.axis_size(a) for a in ALL)
    _, count, side, _ = master.shape
    shards = outers * reps
    plane = shards * cores
    limit = 0.25 * side * math.sqrt(count * plane * plane)
    vmem = pl.BlockSpec(memory_space=pltpu.VMEM)
    smem = pl.BlockSpec(memory_space=pltpu.SMEM)
    hbm = pl.BlockSpec(memory_space=pl.ANY)
    small = pltpu.CompilerParams(vmem_limit_bytes=SMALL)
    large = pltpu.CompilerParams(vmem_limit_bytes=LARGE)
    with jax.named_scope("pick"):
        spread, notes = pl.pallas_call(
            pick_kernel,
            out_shape=(
                jax.ShapeDtypeStruct((shards, SLOTS, side, side), jnp.bfloat16),
                jax.ShapeDtypeStruct((cores * reps, 8, TILE), jnp.float32),
            ),
            in_specs=[hbm, hbm, hbm],
            out_specs=(hbm, vmem),
            scratch_shapes=[
                pltpu.SMEM(keep_mask.shape, keep_mask.dtype),
                pltpu.VMEM(master.shape, master.dtype),
                pltpu.VMEM(synced.shape, synced.dtype),
                pltpu.VMEM((SLOTS, side, side), jnp.bfloat16),
                pltpu.SemaphoreType.DMA((3,)),
                pltpu.SemaphoreType.DMA((shards,)),
            ],
        )(keep_mask, master, synced)
    with jax.named_scope("row_sum"):
        row_sum = pl.pallas_call(
            row_kernel,
            out_shape=jax.ShapeDtypeStruct((8, TILE), jnp.float32),
            in_specs=[vmem],
            out_specs=vmem,
            compiler_params=small,
        )(lax.all_to_all(notes, ROW, 0, 0, tiled=True))
    spread, row_sum = lax.optimization_barrier((spread, row_sum))
    with jax.named_scope("gather"):
        gathered = lax.all_to_all(spread, PEERS, 0, 0, tiled=True)
        gathered = gathered.reshape(shards * SLOTS, side, side)
    with jax.named_scope("z_shift"):
        pairs = []
        for o in range(outers):
            for z in range(chips):
                for c in range(cores):
                    for r in range(reps):
                        there = (z + (o * cores + c) * reps + r - plane // 2 + 1) % chips
                        pairs.append(
                            (((o * chips + z) * cores + c) * reps + r, ((o * chips + there) * cores + c) * reps + r)
                        )
        other = lax.ppermute(lax.psum(row_sum, "outer"), ALL, pairs)
    other, gathered = lax.optimization_barrier((other, gathered))
    with jax.named_scope("plane_sum"):
        notes = pl.pallas_call(
            mix_kernel,
            out_shape=jax.ShapeDtypeStruct((plane, 8, TILE), jnp.float32),
            in_specs=[vmem, vmem],
            out_specs=vmem,
            compiler_params=small,
        )(other, notes)
        notes = lax.all_to_all(notes, PLANE, 0, 0, tiled=True)
        factor, table = pl.pallas_call(
            functools.partial(plane_kernel, limit, outers, reps),
            out_shape=(
                jax.ShapeDtypeStruct((8, TILE), jnp.float32),
                jax.ShapeDtypeStruct((shards, TILE), jnp.int32),
            ),
            in_specs=[vmem],
            out_specs=(vmem, vmem),
            compiler_params=small,
        )(notes)
    with jax.named_scope("apply"):
        return pl.pallas_call(
            functools.partial(apply_kernel, count),
            out_shape=jax.ShapeDtypeStruct(resident.shape, resident.dtype),
            in_specs=[smem, vmem, vmem, hbm],
            out_specs=hbm,
            scratch_shapes=[
                pltpu.VMEM(resident.shape, resident.dtype),
                pltpu.SemaphoreType.DMA((shards,)),
                pltpu.SemaphoreType.DMA((shards,)),
            ],
            compiler_params=large,
        )(table, factor, gathered, resident)


def solution(mesh):
    outers, tensors, reps = mesh.devices.shape
    fine = Mesh(mesh.devices.reshape(outers, tensors // 2, 2, reps), ALL)
    head = ("z", "core")
    placed = (
        P(head, PEERS, None, None),
        P(head, PEERS, None, None),
        P(head, PEERS),
        P(None, head, None),
    )
    return jax.shard_map(
        body, mesh=fine, in_specs=placed, out_specs=P(None, head, None), check_vma=False
    )
```

```python
import functools
import math

import jax
import jax.numpy as jnp
from jax import lax
from jax.experimental import pallas as pl
from jax.experimental.pallas import tpu as pltpu
from jax.sharding import Mesh, PartitionSpec as P

SLOTS = 4
TILE = 128
SMALL = 4 * 2**20
LARGE = 53 * 10**6
ALL = ("outer", "z", "core", "rep")
PLANE = ("outer", "core", "rep")
ROW = ("core", "rep")
PEERS = ("outer", "rep")


def pick_kernel(mask_hbm, master_hbm, synced_hbm, spread_hbm, note_ref, mask_ref, master_ref, synced_ref, tiles_ref, sem, out_sem):
    loads = [
        pltpu.make_async_copy(mask_hbm, mask_ref, sem.at[0]),
        pltpu.make_async_copy(master_hbm, master_ref, sem.at[1]),
        pltpu.make_async_copy(synced_hbm, synced_ref, sem.at[2]),
    ]
    for load in loads:
        load.start()
    loads[0].wait()
    where = [jnp.int32(0)] * SLOTS
    used = jnp.int32(0)
    for i in range(mask_ref.shape[1]):
        listed = mask_ref[0, i] > 0
        for s in range(SLOTS):
            where[s] = jnp.where(listed & (used == s), i, where[s])
        used = used + listed.astype(jnp.int32)
    for load in loads[1:]:
        load.wait()
    squares = jnp.zeros((8, TILE), jnp.float32)
    for s in range(SLOTS):
        delta = (master_ref[0, where[s]] - synced_ref[0, where[s]].astype(jnp.float32)).astype(jnp.bfloat16)
        tiles_ref[s] = delta
        wide = jnp.where(used > s, delta.astype(jnp.float32), 0.0)
        squares = squares + jnp.sum((wide * wide).reshape(-1, 8, TILE), axis=0)
    sends = [
        pltpu.make_async_copy(tiles_ref, spread_hbm.at[j], out_sem.at[j]) for j in range(spread_hbm.shape[0])
    ]
    for send in sends:
        send.start()
    lane = lax.broadcasted_iota(jnp.int32, note_ref.shape[1:], 1)
    note = jnp.where(lane == 0, jnp.sum(squares), 0.0)
    for k, entry in enumerate([used] + where):
        note = jnp.where(lane == 1 + k, entry.astype(jnp.float32), note)
    note_ref[...] = jnp.broadcast_to(note[None], note_ref.shape)
    for send in sends:
        send.wait()


def row_kernel(notes_ref, sum_ref):
    total = jnp.sum(notes_ref[...], axis=0)
    sum_ref[...] = jnp.broadcast_to(total[:, 0:1], total.shape)


def mix_kernel(note_ref, *refs):
    *other_refs, notes_ref = refs
    others = sum(ref[...] for ref in other_refs)
    note = note_ref[0]
    lane = lax.broadcasted_iota(jnp.int32, note.shape, 1)
    note = jnp.where(lane == 0, others, note)
    notes_ref[...] = jnp.broadcast_to(note[None], notes_ref.shape)


def plane_kernel(limit, outers, reps, notes_ref, factor_ref, table_ref):
    core = lax.axis_index("core")
    total = jnp.sum(notes_ref[...], axis=0)
    total = jnp.broadcast_to(total[:, 0:1], total.shape)
    factor_ref[...] = jnp.minimum(jnp.float32(1.0), limit / jnp.sqrt(total))
    lane = lax.broadcasted_iota(jnp.int32, (reps, TILE), 1)
    for y in range(outers):
        mine = notes_ref[pl.ds((y * 2 + core) * reps, reps), 0, :]
        table_ref[y * reps:(y + 1) * reps, :] = jnp.where(lane == 0, 0.0, mine).astype(jnp.int32)


def apply_kernel(count, table_ref, factor_ref, tiles_ref, resident_hbm, out_hbm, rows_ref, in_sem, out_sem):
    shards = table_ref.shape[0]
    wide = count * TILE
    per_layer = resident_hbm.shape[2] // wide

    def block(ref, j):
        return ref.at[j // per_layer, :, pl.ds((j % per_layer) * wide, wide)]

    loads = [pltpu.make_async_copy(block(resident_hbm, j), block(rows_ref, j), in_sem.at[j]) for j in range(shards)]
    stores = [pltpu.make_async_copy(block(rows_ref, j), block(out_hbm, j), out_sem.at[j]) for j in range(shards)]
    for load in loads:
        load.start()
    factor = factor_ref[...][None]
    for j in range(shards):
        loads[j].wait()

        def update(s, _):
            start = pl.multiple_of((j % per_layer) * wide + table_ref[j, 2 + s] * TILE, TILE)
            place = (j // per_layer, slice(None), pl.ds(start, TILE))
            moved = (factor * tiles_ref[j * SLOTS + s].astype(jnp.float32).reshape(-1, 8, TILE)).reshape(TILE, TILE)
            rows_ref[place] = (rows_ref[place].astype(jnp.float32) + moved).astype(jnp.bfloat16)
            return 0

        lax.fori_loop(0, table_ref[j, 1], update, 0)
        stores[j].start()
    for store in stores:
        store.wait()


def body(master, synced, keep_mask, resident):
    outers, chips, cores, reps = (lax.axis_size(a) for a in ALL)
    _, count, side, _ = master.shape
    shards = outers * reps
    plane = shards * cores
    row = cores * reps
    fetches = max(1, chips // row)
    limit = 0.25 * side * math.sqrt(count * plane * row * fetches)
    vmem = pl.BlockSpec(memory_space=pltpu.VMEM)
    smem = pl.BlockSpec(memory_space=pltpu.SMEM)
    hbm = pl.BlockSpec(memory_space=pl.ANY)
    small = pltpu.CompilerParams(vmem_limit_bytes=SMALL)
    large = pltpu.CompilerParams(vmem_limit_bytes=LARGE)
    with jax.named_scope("pick"):
        spread, notes = pl.pallas_call(
            pick_kernel,
            out_shape=(
                jax.ShapeDtypeStruct((shards, SLOTS, side, side), jnp.bfloat16),
                jax.ShapeDtypeStruct((cores * reps, 8, TILE), jnp.float32),
            ),
            in_specs=[hbm, hbm, hbm],
            out_specs=(hbm, vmem),
            scratch_shapes=[
                pltpu.SMEM(keep_mask.shape, keep_mask.dtype),
                pltpu.VMEM(master.shape, master.dtype),
                pltpu.VMEM(synced.shape, synced.dtype),
                pltpu.VMEM((SLOTS, side, side), jnp.bfloat16),
                pltpu.SemaphoreType.DMA((3,)),
                pltpu.SemaphoreType.DMA((shards,)),
            ],
        )(keep_mask, master, synced)
    with jax.named_scope("row_sum"):
        row_sum = pl.pallas_call(
            row_kernel,
            out_shape=jax.ShapeDtypeStruct((8, TILE), jnp.float32),
            in_specs=[vmem],
            out_specs=vmem,
            compiler_params=small,
        )(lax.all_to_all(notes, ROW, 0, 0, tiled=True))
    spread, row_sum = lax.optimization_barrier((spread, row_sum))
    with jax.named_scope("gather"):
        gathered = lax.all_to_all(spread, PEERS, 0, 0, tiled=True)
        gathered = gathered.reshape(shards * SLOTS, side, side)
    with jax.named_scope("z_shift"):
        others = []
        for k in range(fetches):
            pairs = []
            for o in range(outers):
                for z in range(chips):
                    for c in range(cores):
                        for r in range(reps):
                            p = c * reps + r
                            away = k * row // 2 + p // 2 + 1 if p % 2 else -(k * row // 2 + p // 2)
                            there = (z + away) % chips
                            pairs.append(
                                (((o * chips + z) * cores + c) * reps + r, ((o * chips + there) * cores + c) * reps + r)
                            )
            others.append(lax.ppermute(row_sum, ALL, pairs))
    others, gathered = lax.optimization_barrier((others, gathered))
    with jax.named_scope("plane_sum"):
        notes = pl.pallas_call(
            mix_kernel,
            out_shape=jax.ShapeDtypeStruct((plane, 8, TILE), jnp.float32),
            in_specs=[vmem] * (fetches + 1),
            out_specs=vmem,
            compiler_params=small,
        )(notes, *others)
        notes = lax.all_to_all(notes, PLANE, 0, 0, tiled=True)
        factor, table = pl.pallas_call(
            functools.partial(plane_kernel, limit, outers, reps),
            out_shape=(
                jax.ShapeDtypeStruct((8, TILE), jnp.float32),
                jax.ShapeDtypeStruct((shards, TILE), jnp.int32),
            ),
            in_specs=[vmem],
            out_specs=(vmem, vmem),
            compiler_params=small,
        )(notes)
    with jax.named_scope("apply"):
        return pl.pallas_call(
            functools.partial(apply_kernel, count),
            out_shape=jax.ShapeDtypeStruct(resident.shape, resident.dtype),
            in_specs=[smem, vmem, vmem, hbm],
            out_specs=hbm,
            scratch_shapes=[
                pltpu.VMEM(resident.shape, resident.dtype),
                pltpu.SemaphoreType.DMA((shards,)),
                pltpu.SemaphoreType.DMA((shards,)),
            ],
            compiler_params=large,
        )(table, factor, gathered, resident)


def solution(mesh):
    outers, tensors, reps = mesh.devices.shape
    fine = Mesh(mesh.devices.reshape(outers, tensors // 2, 2, reps), ALL)
    head = ("z", "core")
    placed = (
        P(head, PEERS, None, None),
        P(head, PEERS, None, None),
        P(head, PEERS),
        P(None, head, None),
    )
    return jax.shard_map(
        body, mesh=fine, in_specs=placed, out_specs=P(None, head, None), check_vma=False
    )
```

```python
import functools
import math

import jax
import jax.numpy as jnp
from jax import lax
from jax.experimental import pallas as pl
from jax.experimental.pallas import tpu as pltpu
from jax.sharding import Mesh, PartitionSpec as P

SLOTS = 4
TILE = 128
SMALL = 4 * 2**20
LARGE = 53 * 10**6
PICK = 568 * 10**5
ALL = ("outer", "z", "core", "rep")
PLANE = ("outer", "core", "rep")
PEERS = ("outer", "rep")


def pick_kernel(mask_hbm, master_hbm, synced_hbm, spread_hbm, notes_ref, mask_ref, master_ref, synced_ref, tiles_ref, sem, out_sem):
    loads = [
        pltpu.make_async_copy(mask_hbm, mask_ref, sem.at[0]),
        pltpu.make_async_copy(master_hbm, master_ref, sem.at[1]),
        pltpu.make_async_copy(synced_hbm, synced_ref, sem.at[2]),
    ]
    for load in loads:
        load.start()
    loads[0].wait()
    where = [jnp.int32(0)] * SLOTS
    used = jnp.int32(0)
    for i in range(mask_ref.shape[1]):
        listed = mask_ref[0, i] > 0
        for s in range(SLOTS):
            where[s] = jnp.where(listed & (used == s), i, where[s])
        used = used + listed.astype(jnp.int32)
    for load in loads[1:]:
        load.wait()
    squares = jnp.zeros((8, TILE), jnp.float32)
    for s in range(SLOTS):
        delta = (master_ref[0, where[s]] - synced_ref[0, where[s]].astype(jnp.float32)).astype(jnp.bfloat16)
        tiles_ref[s] = delta
        wide = jnp.where(used > s, delta.astype(jnp.float32), 0.0)
        squares = squares + jnp.sum((wide * wide).reshape(-1, 8, TILE), axis=0)
    sends = [
        pltpu.make_async_copy(tiles_ref, spread_hbm.at[j], out_sem.at[j]) for j in range(spread_hbm.shape[0])
    ]
    for send in sends:
        send.start()
    lane = lax.broadcasted_iota(jnp.int32, notes_ref.shape[1:], 1)
    note = jnp.where(lane == 0, jnp.sum(squares), 0.0)
    for k, entry in enumerate([used] + where):
        note = jnp.where(lane == 1 + k, entry.astype(jnp.float32), note)
    notes_ref[...] = jnp.broadcast_to(note[None], notes_ref.shape)
    for send in sends:
        send.wait()


def plane_kernel(outers, reps, notes_ref, sum_ref, table_ref):
    core = lax.axis_index("core")
    total = jnp.sum(notes_ref[...], axis=0)
    sum_ref[...] = jnp.broadcast_to(total[:, 0:1], total.shape)
    lane = lax.broadcasted_iota(jnp.int32, (reps, TILE), 1)
    for y in range(outers):
        mine = notes_ref[pl.ds((y * 2 + core) * reps, reps), 0, :]
        table_ref[y * reps:(y + 1) * reps, :] = jnp.where(lane == 0, 0.0, mine).astype(jnp.int32)


def apply_kernel(limit, count, table_ref, sums_ref, tiles_ref, resident_hbm, out_hbm, rows_ref, in_sem, out_sem):
    shards = table_ref.shape[0]
    wide = count * TILE
    per_layer = resident_hbm.shape[2] // wide

    def block(ref, j):
        return ref.at[j // per_layer, :, pl.ds((j % per_layer) * wide, wide)]

    loads = [pltpu.make_async_copy(block(resident_hbm, j), block(rows_ref, j), in_sem.at[j]) for j in range(shards)]
    stores = [pltpu.make_async_copy(block(rows_ref, j), block(out_hbm, j), out_sem.at[j]) for j in range(shards)]
    for load in loads:
        load.start()
    total = jnp.sum(sums_ref[...], axis=0)
    factor = jnp.minimum(jnp.float32(1.0), limit / jnp.sqrt(total))[None]
    for j in range(shards):
        loads[j].wait()

        def update(s, _):
            start = pl.multiple_of((j % per_layer) * wide + table_ref[j, 2 + s] * TILE, TILE)
            place = (j // per_layer, slice(None), pl.ds(start, TILE))
            moved = (factor * tiles_ref[j * SLOTS + s].astype(jnp.float32).reshape(-1, 8, TILE)).reshape(TILE, TILE)
            rows_ref[place] = (rows_ref[place].astype(jnp.float32) + moved).astype(jnp.bfloat16)
            return 0

        lax.fori_loop(0, table_ref[j, 1], update, 0)
        stores[j].start()
    for store in stores:
        store.wait()


def body(master, synced, keep_mask, resident):
    outers, chips, cores, reps = (lax.axis_size(a) for a in ALL)
    _, count, side, _ = master.shape
    shards = outers * reps
    plane = shards * cores
    vmem = pl.BlockSpec(memory_space=pltpu.VMEM)
    smem = pl.BlockSpec(memory_space=pltpu.SMEM)
    hbm = pl.BlockSpec(memory_space=pl.ANY)
    small = pltpu.CompilerParams(vmem_limit_bytes=SMALL)
    large = pltpu.CompilerParams(vmem_limit_bytes=LARGE)
    with jax.named_scope("pick"):
        spread, notes = pl.pallas_call(
            pick_kernel,
            out_shape=(
                jax.ShapeDtypeStruct((shards, SLOTS, side, side), jnp.bfloat16),
                jax.ShapeDtypeStruct((plane, 8, TILE), jnp.float32),
            ),
            in_specs=[hbm, hbm, hbm],
            out_specs=(hbm, vmem),
            scratch_shapes=[
                pltpu.SMEM(keep_mask.shape, keep_mask.dtype),
                pltpu.VMEM(master.shape, master.dtype),
                pltpu.VMEM(synced.shape, synced.dtype),
                pltpu.VMEM((SLOTS, side, side), jnp.bfloat16),
                pltpu.SemaphoreType.DMA((3,)),
                pltpu.SemaphoreType.DMA((shards,)),
            ],
            compiler_params=pltpu.CompilerParams(vmem_limit_bytes=PICK),
        )(keep_mask, master, synced)
    with jax.named_scope("plane_sum"):
        notes = lax.all_to_all(notes, PLANE, 0, 0, tiled=True)
        plane_total, table = pl.pallas_call(
            functools.partial(plane_kernel, outers, reps),
            out_shape=(
                jax.ShapeDtypeStruct((8, TILE), jnp.float32),
                jax.ShapeDtypeStruct((shards, TILE), jnp.int32),
            ),
            in_specs=[vmem],
            out_specs=(vmem, vmem),
            compiler_params=small,
        )(notes)
    spread, plane_total = lax.optimization_barrier((spread, plane_total))
    with jax.named_scope("gather"):
        gathered = lax.all_to_all(spread, PEERS, 0, 0, tiled=True)
        gathered = gathered.reshape(shards * SLOTS, side, side)
    with jax.named_scope("z_shift"):
        pairs = []
        for o in range(outers):
            for z in range(chips):
                for c in range(cores):
                    for r in range(reps):
                        there = (z + (o * cores + c) * reps + r - plane // 2 + 1) % chips
                        pairs.append(
                            (((o * chips + z) * cores + c) * reps + r, ((o * chips + there) * cores + c) * reps + r)
                        )
        other = lax.ppermute(plane_total, ALL, pairs)
    other, gathered = lax.optimization_barrier((other, gathered))
    with jax.named_scope("z_sum"):
        sums = lax.all_to_all(jnp.broadcast_to(other[None], (plane, 8, TILE)), PLANE, 0, 0, tiled=True)
    limit = 0.25 * side * math.sqrt(count * plane * chips)
    limit = limit * math.sqrt(plane / chips)
    with jax.named_scope("apply"):
        return pl.pallas_call(
            functools.partial(apply_kernel, limit, count),
            out_shape=jax.ShapeDtypeStruct(resident.shape, resident.dtype),
            in_specs=[smem, vmem, vmem, hbm],
            out_specs=hbm,
            scratch_shapes=[
                pltpu.VMEM(resident.shape, resident.dtype),
                pltpu.SemaphoreType.DMA((shards,)),
                pltpu.SemaphoreType.DMA((shards,)),
            ],
            compiler_params=large,
        )(table, sums, gathered, resident)


def solution(mesh):
    outers, tensors, reps = mesh.devices.shape
    fine = Mesh(mesh.devices.reshape(outers, tensors // 2, 2, reps), ALL)
    head = ("z", "core")
    placed = (
        P(head, PEERS, None, None),
        P(head, PEERS, None, None),
        P(head, PEERS),
        P(None, head, None),
    )
    return jax.shard_map(
        body, mesh=fine, in_specs=placed, out_specs=P(None, head, None), check_vma=False
    )
```

```python
import functools
import math

import jax
import jax.numpy as jnp
from jax import lax
from jax.experimental import pallas as pl
from jax.experimental.pallas import tpu as pltpu
from jax.sharding import Mesh, PartitionSpec as P

SLOTS = 4
LATER = SLOTS - 1
TILE = 128
SMALL = 4 * 2**20
LARGE = 53 * 10**6
PICK = 568 * 10**5
ALL = ("outer", "z", "core", "rep")
PLANE = ("outer", "core", "rep")
PEERS = ("outer", "rep")


def pick_kernel(
    mask_hbm, master_hbm, synced_hbm, first_hbm, later_hbm, mask_ref, master_ref, synced_ref, first_ref, later_ref, sem, out_sem
):
    shards = later_hbm.shape[0]
    loads = [
        pltpu.make_async_copy(mask_hbm, mask_ref, sem.at[0]),
        pltpu.make_async_copy(master_hbm, master_ref, sem.at[1]),
        pltpu.make_async_copy(synced_hbm, synced_ref, sem.at[2]),
    ]
    for load in loads:
        load.start()
    loads[0].wait()
    where = [jnp.int32(0)] * SLOTS
    used = jnp.int32(0)
    for i in range(mask_ref.shape[1]):
        listed = mask_ref[0, i] > 0
        for s in range(SLOTS):
            where[s] = jnp.where(listed & (used == s), i, where[s])
        used = used + listed.astype(jnp.int32)
    for load in loads[1:]:
        load.wait()
    squares = jnp.zeros((8, TILE), jnp.float32)
    for s in range(SLOTS):
        delta = (master_ref[0, where[s]] - synced_ref[0, where[s]].astype(jnp.float32)).astype(jnp.bfloat16)
        if s == 0:
            first_ref[0:TILE] = delta
        else:
            later_ref[s - 1] = delta
        wide = jnp.where(used > s, delta.astype(jnp.float32), 0.0)
        squares = squares + jnp.sum((wide * wide).reshape(-1, 8, TILE), axis=0)
    sends = [pltpu.make_async_copy(later_ref, later_hbm.at[j], out_sem.at[0, j]) for j in range(shards)]
    for send in sends:
        send.start()
    lane = lax.broadcasted_iota(jnp.int32, (16, TILE), 1)
    total = jnp.full((16, TILE), jnp.sum(squares), jnp.float32)
    high = total.astype(jnp.bfloat16).astype(jnp.float32)
    middle = (total - high).astype(jnp.bfloat16).astype(jnp.float32)
    low = total - high - middle
    note = jnp.where(lane == 0, high, jnp.where(lane == 8, middle, jnp.where(lane == 9, low, 0.0)))
    for k, entry in enumerate([used] + where):
        note = jnp.where(lane == 1 + k, entry.astype(jnp.float32), note)
    first_ref[TILE:TILE + 16] = note.astype(jnp.bfloat16)
    firsts = [pltpu.make_async_copy(first_ref, first_hbm.at[j], out_sem.at[1, j]) for j in range(shards)]
    for send in firsts:
        send.start()
    for send in sends + firsts:
        send.wait()


def plane_kernel(first_ref, sum_ref, table_ref):
    shards = first_ref.shape[0]
    lane = lax.broadcasted_iota(jnp.int32, (16, TILE), 1)
    part = (lane == 0) | (lane == 8) | (lane == 9)
    total = jnp.zeros((16, TILE), jnp.float32)
    for j in range(shards):
        note = first_ref[j, TILE:TILE + 16].astype(jnp.float32)
        total = total + jnp.sum(jnp.where(part, note, 0.0), axis=1, keepdims=True)
        table_ref[j:j + 1, :] = jnp.where(part, 0.0, note)[0:1].astype(jnp.int32)
    sum_ref[...] = total[0:8]


def apply_kernel(
    limit, count, table_ref, sums_ref, first_hbm, later_ref, resident_hbm, out_hbm, rows_ref, first_ref, in_sem, first_sem, out_sem
):
    shards = table_ref.shape[0]
    wide = count * TILE
    per_layer = resident_hbm.shape[2] // wide

    def block(ref, j):
        return ref.at[j // per_layer, :, pl.ds((j % per_layer) * wide, wide)]

    loads = [pltpu.make_async_copy(block(resident_hbm, j), block(rows_ref, j), in_sem.at[j]) for j in range(shards)]
    firsts = [
        pltpu.make_async_copy(first_hbm.at[j, pl.ds(0, TILE)], first_ref.at[j], first_sem.at[j]) for j in range(shards)
    ]
    stores = [pltpu.make_async_copy(block(rows_ref, j), block(out_hbm, j), out_sem.at[j]) for j in range(shards)]
    for first, load in zip(firsts, loads):
        first.start()
        load.start()
    total = jnp.sum(sums_ref[...], axis=0)
    factor = jnp.minimum(jnp.float32(1.0), limit / jnp.sqrt(total))[None]
    for j in range(shards):
        firsts[j].wait()
        loads[j].wait()

        def add(slot, tile):
            start = pl.multiple_of((j % per_layer) * wide + table_ref[j, 2 + slot] * TILE, TILE)
            place = (j // per_layer, slice(None), pl.ds(start, TILE))
            moved = (factor * tile.astype(jnp.float32).reshape(-1, 8, TILE)).reshape(TILE, TILE)
            rows_ref[place] = (rows_ref[place].astype(jnp.float32) + moved).astype(jnp.bfloat16)

        @pl.when(table_ref[j, 1] > 0)
        def _():
            add(0, first_ref[j])

        def later(s, _):
            add(s, later_ref[j * LATER + s - 1])
            return 0

        lax.fori_loop(1, table_ref[j, 1], later, 0)
        stores[j].start()
    for store in stores:
        store.wait()


def body(master, synced, keep_mask, resident):
    outers, chips, cores, reps = (lax.axis_size(a) for a in ALL)
    _, count, side, _ = master.shape
    shards = outers * reps
    plane = shards * cores
    fetches = max(1, chips // shards)
    limit = 0.25 * side * math.sqrt(count * plane * shards * fetches)
    vmem = pl.BlockSpec(memory_space=pltpu.VMEM)
    smem = pl.BlockSpec(memory_space=pltpu.SMEM)
    hbm = pl.BlockSpec(memory_space=pl.ANY)
    small = pltpu.CompilerParams(vmem_limit_bytes=SMALL)
    large = pltpu.CompilerParams(vmem_limit_bytes=LARGE)
    with jax.named_scope("pick"):
        first, later = pl.pallas_call(
            pick_kernel,
            out_shape=(
                jax.ShapeDtypeStruct((shards, side + 16, side), jnp.bfloat16),
                jax.ShapeDtypeStruct((shards, LATER, side, side), jnp.bfloat16),
            ),
            in_specs=[hbm, hbm, hbm],
            out_specs=(hbm, hbm),
            scratch_shapes=[
                pltpu.SMEM(keep_mask.shape, keep_mask.dtype),
                pltpu.VMEM(master.shape, master.dtype),
                pltpu.VMEM(synced.shape, synced.dtype),
                pltpu.VMEM((side + 16, side), jnp.bfloat16),
                pltpu.VMEM((LATER, side, side), jnp.bfloat16),
                pltpu.SemaphoreType.DMA((3,)),
                pltpu.SemaphoreType.DMA((2, shards)),
            ],
        )(keep_mask, master, synced)
    with jax.named_scope("first_slot"):
        first = lax.all_to_all(first, PEERS, 0, 0, tiled=True)
        plane_sum, table = pl.pallas_call(
            plane_kernel,
            out_shape=(
                jax.ShapeDtypeStruct((8, TILE), jnp.float32),
                jax.ShapeDtypeStruct((shards, TILE), jnp.int32),
            ),
            in_specs=[vmem],
            out_specs=(vmem, vmem),
            compiler_params=small,
        )(first)
    later, plane_sum = lax.optimization_barrier((later, plane_sum))
    with jax.named_scope("later_slots"):
        later = lax.all_to_all(later, PEERS, 0, 0, tiled=True)
        later = later.reshape(shards * LATER, side, side)
    with jax.named_scope("z_shift"):
        others = []
        for k in range(fetches):
            pairs = []
            for o in range(outers):
                for z in range(chips):
                    for c in range(cores):
                        for r in range(reps):
                            p = o * reps + r
                            away = k * shards // 2 + p // 2 + 1 if p % 2 else -(k * shards // 2 + p // 2)
                            there = (z + away) % chips
                            pairs.append(
                                (((o * chips + z) * cores + c) * reps + r, ((o * chips + there) * cores + c) * reps + r)
                            )
            others.append(lax.ppermute(plane_sum, ALL, pairs))
    others, later = lax.optimization_barrier((others, later))
    with jax.named_scope("z_sum"):
        sums = lax.all_to_all(jnp.broadcast_to(sum(others)[None], (plane, 8, TILE)), PLANE, 0, 0, tiled=True)
    with jax.named_scope("apply"):
        return pl.pallas_call(
            functools.partial(apply_kernel, limit, count),
            out_shape=jax.ShapeDtypeStruct(resident.shape, resident.dtype),
            in_specs=[smem, vmem, hbm, vmem, hbm],
            out_specs=hbm,
            scratch_shapes=[
                pltpu.VMEM(resident.shape, resident.dtype),
                pltpu.VMEM((shards, side, side), jnp.bfloat16),
                pltpu.SemaphoreType.DMA((shards,)),
                pltpu.SemaphoreType.DMA((shards,)),
                pltpu.SemaphoreType.DMA((shards,)),
            ],
            compiler_params=large,
        )(table, sums, first, later, resident)


def solution(mesh):
    outers, tensors, reps = mesh.devices.shape
    fine = Mesh(mesh.devices.reshape(outers, tensors // 2, 2, reps), ALL)
    head = ("z", "core")
    placed = (
        P(head, PEERS, None, None),
        P(head, PEERS, None, None),
        P(head, PEERS),
        P(None, head, None),
    )
    return jax.shard_map(
        body, mesh=fine, in_specs=placed, out_specs=P(None, head, None), check_vma=False
    )
```

```python
import functools
import math

import jax
import jax.numpy as jnp
from jax import lax
from jax.experimental import pallas as pl
from jax.experimental.pallas import tpu as pltpu
from jax.sharding import Mesh, PartitionSpec as P

SLOTS = 4
LATER = SLOTS - 1
TILE = 128
SMALL = 4 * 2**20
LARGE = 53 * 10**6
PICK = 568 * 10**5
ALL = ("outer", "z", "core", "rep")
PLANE = ("outer", "core", "rep")
PEERS = ("outer", "rep")


def pick_kernel(
    mask_hbm, master_hbm, synced_hbm, first_hbm, later_hbm, mask_ref, master_ref, synced_ref, first_ref, later_ref, sem, out_sem
):
    shards = later_hbm.shape[0]
    loads = [
        pltpu.make_async_copy(mask_hbm, mask_ref, sem.at[0]),
        pltpu.make_async_copy(master_hbm, master_ref, sem.at[1]),
        pltpu.make_async_copy(synced_hbm, synced_ref, sem.at[2]),
    ]
    for load in loads:
        load.start()
    loads[0].wait()
    where = [jnp.int32(0)] * SLOTS
    used = jnp.int32(0)
    for i in range(mask_ref.shape[1]):
        listed = mask_ref[0, i] > 0
        for s in range(SLOTS):
            where[s] = jnp.where(listed & (used == s), i, where[s])
        used = used + listed.astype(jnp.int32)
    for load in loads[1:]:
        load.wait()
    squares = jnp.zeros((8, TILE), jnp.float32)
    for s in range(SLOTS):
        delta = (master_ref[0, where[s]] - synced_ref[0, where[s]].astype(jnp.float32)).astype(jnp.bfloat16)
        if s == 0:
            first_ref[0:TILE] = delta
        else:
            later_ref[s - 1] = delta
        wide = jnp.where(used > s, delta.astype(jnp.float32), 0.0)
        squares = squares + jnp.sum((wide * wide).reshape(-1, 8, TILE), axis=0)
    sends = [pltpu.make_async_copy(later_ref, later_hbm.at[j], out_sem.at[0, j]) for j in range(shards)]
    for send in sends:
        send.start()
    lane = lax.broadcasted_iota(jnp.int32, (16, TILE), 1)
    total = jnp.full((16, TILE), jnp.sum(squares), jnp.float32)
    high = total.astype(jnp.bfloat16).astype(jnp.float32)
    middle = (total - high).astype(jnp.bfloat16).astype(jnp.float32)
    low = total - high - middle
    note = jnp.where(lane == 0, high, jnp.where(lane == 8, middle, jnp.where(lane == 9, low, 0.0)))
    for k, entry in enumerate([used] + where):
        note = jnp.where(lane == 1 + k, entry.astype(jnp.float32), note)
    first_ref[TILE:TILE + 16] = note.astype(jnp.bfloat16)
    firsts = [pltpu.make_async_copy(first_ref, first_hbm.at[j], out_sem.at[1, j]) for j in range(shards)]
    for send in firsts:
        send.start()
    for send in sends + firsts:
        send.wait()


def plane_kernel(first_ref, sum_ref, table_ref):
    shards = first_ref.shape[0]
    lane = lax.broadcasted_iota(jnp.int32, (16, TILE), 1)
    part = (lane == 0) | (lane == 8) | (lane == 9)
    total = jnp.zeros((16, TILE), jnp.float32)
    for j in range(shards):
        note = first_ref[j, TILE:TILE + 16].astype(jnp.float32)
        total = total + jnp.sum(jnp.where(part, note, 0.0), axis=1, keepdims=True)
        table_ref[j:j + 1, :] = jnp.where(part, 0.0, note)[0:1].astype(jnp.int32)
    sum_ref[...] = total[0:8]


def apply_kernel(
    limit, count, table_ref, sums_ref, first_hbm, later_ref, resident_hbm, out_hbm, rows_ref, first_ref, in_sem, first_sem, out_sem
):
    shards = table_ref.shape[0]
    wide = count * TILE
    per_layer = resident_hbm.shape[2] // wide

    def block(ref, j):
        return ref.at[j // per_layer, :, pl.ds((j % per_layer) * wide, wide)]

    loads = [pltpu.make_async_copy(block(resident_hbm, j), block(rows_ref, j), in_sem.at[j]) for j in range(shards)]
    firsts = [
        pltpu.make_async_copy(first_hbm.at[j, pl.ds(0, TILE)], first_ref.at[j], first_sem.at[j]) for j in range(shards)
    ]
    stores = [pltpu.make_async_copy(block(rows_ref, j), block(out_hbm, j), out_sem.at[j]) for j in range(shards)]
    for first, load in zip(firsts, loads):
        first.start()
        load.start()
    total = jnp.sum(sums_ref[...], axis=0)
    factor = jnp.minimum(jnp.float32(1.0), limit / jnp.sqrt(total))[None]
    for j in range(shards):
        firsts[j].wait()
        loads[j].wait()

        def add(slot, tile):
            start = pl.multiple_of((j % per_layer) * wide + table_ref[j, 2 + slot] * TILE, TILE)
            place = (j // per_layer, slice(None), pl.ds(start, TILE))
            moved = (factor * tile.astype(jnp.float32).reshape(-1, 8, TILE)).reshape(TILE, TILE)
            rows_ref[place] = (rows_ref[place].astype(jnp.float32) + moved).astype(jnp.bfloat16)

        @pl.when(table_ref[j, 1] > 0)
        def _():
            add(0, first_ref[j])

        def later(s, _):
            add(s, later_ref[j * LATER + s - 1])
            return 0

        lax.fori_loop(1, table_ref[j, 1], later, 0)
        stores[j].start()
    for store in stores:
        store.wait()


def body(master, synced, keep_mask, resident):
    outers, chips, cores, reps = (lax.axis_size(a) for a in ALL)
    _, count, side, _ = master.shape
    shards = outers * reps
    plane = shards * cores
    limit = 0.25 * side * math.sqrt(count * plane * plane)
    vmem = pl.BlockSpec(memory_space=pltpu.VMEM)
    smem = pl.BlockSpec(memory_space=pltpu.SMEM)
    hbm = pl.BlockSpec(memory_space=pl.ANY)
    small = pltpu.CompilerParams(vmem_limit_bytes=SMALL)
    large = pltpu.CompilerParams(vmem_limit_bytes=LARGE)
    with jax.named_scope("pick"):
        first, later = pl.pallas_call(
            pick_kernel,
            out_shape=(
                jax.ShapeDtypeStruct((shards, side + 16, side), jnp.bfloat16),
                jax.ShapeDtypeStruct((shards, LATER, side, side), jnp.bfloat16),
            ),
            in_specs=[hbm, hbm, hbm],
            out_specs=(hbm, hbm),
            scratch_shapes=[
                pltpu.SMEM(keep_mask.shape, keep_mask.dtype),
                pltpu.VMEM(master.shape, master.dtype),
                pltpu.VMEM(synced.shape, synced.dtype),
                pltpu.VMEM((side + 16, side), jnp.bfloat16),
                pltpu.VMEM((LATER, side, side), jnp.bfloat16),
                pltpu.SemaphoreType.DMA((3,)),
                pltpu.SemaphoreType.DMA((2, shards)),
            ],
        )(keep_mask, master, synced)
    with jax.named_scope("first_slot"):
        first = lax.all_to_all(first, PEERS, 0, 0, tiled=True)
        plane_sum, table = pl.pallas_call(
            plane_kernel,
            out_shape=(
                jax.ShapeDtypeStruct((8, TILE), jnp.float32),
                jax.ShapeDtypeStruct((shards, TILE), jnp.int32),
            ),
            in_specs=[vmem],
            out_specs=(vmem, vmem),
            compiler_params=small,
        )(first)
        plane_sum = lax.psum(plane_sum, "core")
    later, plane_sum = lax.optimization_barrier((later, plane_sum))
    with jax.named_scope("later_slots"):
        later = lax.all_to_all(later, PEERS, 0, 0, tiled=True)
        later = later.reshape(shards * LATER, side, side)
    with jax.named_scope("z_shift"):
        pairs = []
        for o in range(outers):
            for z in range(chips):
                for c in range(cores):
                    for r in range(reps):
                        there = (z + (o * cores + c) * reps + r - plane // 2 + 1) % chips
                        pairs.append(
                            (((o * chips + z) * cores + c) * reps + r, ((o * chips + there) * cores + c) * reps + r)
                        )
        other = lax.ppermute(plane_sum, ALL, pairs)
    other, later = lax.optimization_barrier((other, later))
    with jax.named_scope("z_sum"):
        sums = lax.all_to_all(jnp.broadcast_to(other[None], (plane, 8, TILE)), PLANE, 0, 0, tiled=True)
    with jax.named_scope("apply"):
        return pl.pallas_call(
            functools.partial(apply_kernel, limit, count),
            out_shape=jax.ShapeDtypeStruct(resident.shape, resident.dtype),
            in_specs=[smem, vmem, hbm, vmem, hbm],
            out_specs=hbm,
            scratch_shapes=[
                pltpu.VMEM(resident.shape, resident.dtype),
                pltpu.VMEM((shards, side, side), jnp.bfloat16),
                pltpu.SemaphoreType.DMA((shards,)),
                pltpu.SemaphoreType.DMA((shards,)),
                pltpu.SemaphoreType.DMA((shards,)),
            ],
            compiler_params=large,
        )(table, sums, first, later, resident)


def solution(mesh):
    outers, tensors, reps = mesh.devices.shape
    fine = Mesh(mesh.devices.reshape(outers, tensors // 2, 2, reps), ALL)
    head = ("z", "core")
    placed = (
        P(head, PEERS, None, None),
        P(head, PEERS, None, None),
        P(head, PEERS),
        P(None, head, None),
    )
    return jax.shard_map(
        body, mesh=fine, in_specs=placed, out_specs=P(None, head, None), check_vma=False
    )
```

```python
import functools
import math

import jax
import jax.numpy as jnp
from jax import lax
from jax.experimental import pallas as pl
from jax.experimental.pallas import tpu as pltpu
from jax.sharding import Mesh, PartitionSpec as P

SLOTS = 4
LATER = SLOTS - 1
TILE = 128
SMALL = 4 * 2**20
LARGE = 53 * 10**6
PICK = 568 * 10**5
ALL = ("outer", "z", "core", "rep")
PLANE = ("outer", "core", "rep")
PEERS = ("outer", "rep")


def pick_kernel(
    mask_hbm, master_hbm, synced_hbm, first_hbm, later_hbm, mask_ref, master_ref, synced_ref, first_ref, later_ref, sem, out_sem
):
    shards = later_hbm.shape[0]
    loads = [
        pltpu.make_async_copy(mask_hbm, mask_ref, sem.at[0]),
        pltpu.make_async_copy(master_hbm, master_ref, sem.at[1]),
        pltpu.make_async_copy(synced_hbm, synced_ref, sem.at[2]),
    ]
    for load in loads:
        load.start()
    loads[0].wait()
    where = [jnp.int32(0)] * SLOTS
    used = jnp.int32(0)
    for i in range(mask_ref.shape[1]):
        listed = mask_ref[0, i] > 0
        for s in range(SLOTS):
            where[s] = jnp.where(listed & (used == s), i, where[s])
        used = used + listed.astype(jnp.int32)
    for load in loads[1:]:
        load.wait()
    squares = jnp.zeros((8, TILE), jnp.float32)
    for s in range(SLOTS):
        delta = (master_ref[0, where[s]] - synced_ref[0, where[s]].astype(jnp.float32)).astype(jnp.bfloat16)
        if s == 0:
            first_ref[0:TILE] = delta
        else:
            later_ref[s - 1] = delta
        wide = jnp.where(used > s, delta.astype(jnp.float32), 0.0)
        squares = squares + jnp.sum((wide * wide).reshape(-1, 8, TILE), axis=0)
    sends = [pltpu.make_async_copy(later_ref, later_hbm.at[j], out_sem.at[0, j]) for j in range(shards)]
    for send in sends:
        send.start()
    lane = lax.broadcasted_iota(jnp.int32, (16, TILE), 1)
    total = jnp.full((16, TILE), jnp.sum(squares), jnp.float32)
    high = total.astype(jnp.bfloat16).astype(jnp.float32)
    middle = (total - high).astype(jnp.bfloat16).astype(jnp.float32)
    low = total - high - middle
    note = jnp.where(lane == 0, high, jnp.where(lane == 8, middle, jnp.where(lane == 9, low, 0.0)))
    for k, entry in enumerate([used] + where):
        note = jnp.where(lane == 1 + k, entry.astype(jnp.float32), note)
    first_ref[TILE:TILE + 16] = note.astype(jnp.bfloat16)
    firsts = [pltpu.make_async_copy(first_ref, first_hbm.at[j], out_sem.at[1, j]) for j in range(shards)]
    for send in firsts:
        send.start()
    for send in sends + firsts:
        send.wait()


def plane_kernel(first_ref, sum_ref, table_ref):
    shards = first_ref.shape[0]
    lane = lax.broadcasted_iota(jnp.int32, (16, TILE), 1)
    part = (lane == 0) | (lane == 8) | (lane == 9)
    total = jnp.zeros((16, TILE), jnp.float32)
    for j in range(shards):
        note = first_ref[j, TILE:TILE + 16].astype(jnp.float32)
        total = total + jnp.sum(jnp.where(part, note, 0.0), axis=1, keepdims=True)
        table_ref[j:j + 1, :] = jnp.where(part, 0.0, note)[0:1].astype(jnp.int32)
    sum_ref[...] = total[0:8]


def apply_kernel(
    limit, count, table_ref, sums_ref, first_ref, later_ref, resident_hbm, out_hbm, rows_ref, in_sem, out_sem
):
    shards = table_ref.shape[0]
    wide = count * TILE
    per_layer = resident_hbm.shape[2] // wide

    def block(ref, j):
        return ref.at[j // per_layer, :, pl.ds((j % per_layer) * wide, wide)]

    loads = [pltpu.make_async_copy(block(resident_hbm, j), block(rows_ref, j), in_sem.at[j]) for j in range(shards)]
    stores = [pltpu.make_async_copy(block(rows_ref, j), block(out_hbm, j), out_sem.at[j]) for j in range(shards)]
    for load in loads:
        load.start()
    total = jnp.sum(sums_ref[...], axis=0)
    factor = jnp.minimum(jnp.float32(1.0), limit / jnp.sqrt(total))[None]
    for j in range(shards):
        loads[j].wait()

        def add(slot, tile):
            start = pl.multiple_of((j % per_layer) * wide + table_ref[j, 2 + slot] * TILE, TILE)
            place = (j // per_layer, slice(None), pl.ds(start, TILE))
            moved = (factor * tile.astype(jnp.float32).reshape(-1, 8, TILE)).reshape(TILE, TILE)
            rows_ref[place] = (rows_ref[place].astype(jnp.float32) + moved).astype(jnp.bfloat16)

        @pl.when(table_ref[j, 1] > 0)
        def _():
            add(0, first_ref[j, 0:TILE])

        def later(s, _):
            add(s, later_ref[j * LATER + s - 1])
            return 0

        lax.fori_loop(1, table_ref[j, 1], later, 0)
        stores[j].start()
    for store in stores:
        store.wait()


def body(master, synced, keep_mask, resident):
    outers, chips, cores, reps = (lax.axis_size(a) for a in ALL)
    _, count, side, _ = master.shape
    shards = outers * reps
    plane = shards * cores
    limit = 0.25 * side * math.sqrt(count * plane * plane)
    vmem = pl.BlockSpec(memory_space=pltpu.VMEM)
    smem = pl.BlockSpec(memory_space=pltpu.SMEM)
    hbm = pl.BlockSpec(memory_space=pl.ANY)
    small = pltpu.CompilerParams(vmem_limit_bytes=SMALL)
    large = pltpu.CompilerParams(vmem_limit_bytes=LARGE)
    with jax.named_scope("pick"):
        first, later = pl.pallas_call(
            pick_kernel,
            out_shape=(
                jax.ShapeDtypeStruct((shards, side + 16, side), jnp.bfloat16),
                jax.ShapeDtypeStruct((shards, LATER, side, side), jnp.bfloat16),
            ),
            in_specs=[hbm, hbm, hbm],
            out_specs=(hbm, hbm),
            scratch_shapes=[
                pltpu.SMEM(keep_mask.shape, keep_mask.dtype),
                pltpu.VMEM(master.shape, master.dtype),
                pltpu.VMEM(synced.shape, synced.dtype),
                pltpu.VMEM((side + 16, side), jnp.bfloat16),
                pltpu.VMEM((LATER, side, side), jnp.bfloat16),
                pltpu.SemaphoreType.DMA((3,)),
                pltpu.SemaphoreType.DMA((2, shards)),
            ],
        )(keep_mask, master, synced)
    with jax.named_scope("first_slot"):
        first = lax.all_to_all(first, PEERS, 0, 0, tiled=True)
        plane_sum, table = pl.pallas_call(
            plane_kernel,
            out_shape=(
                jax.ShapeDtypeStruct((8, TILE), jnp.float32),
                jax.ShapeDtypeStruct((shards, TILE), jnp.int32),
            ),
            in_specs=[vmem],
            out_specs=(vmem, vmem),
            compiler_params=small,
        )(first)
    later, plane_sum = lax.optimization_barrier((later, plane_sum))
    with jax.named_scope("later_slots"):
        later = lax.all_to_all(later, PEERS, 0, 0, tiled=True)
        later = later.reshape(shards * LATER, side, side)
    with jax.named_scope("z_shift"):
        pairs = []
        for o in range(outers):
            for z in range(chips):
                for c in range(cores):
                    for r in range(reps):
                        there = (z + (o * cores + c) * reps + r - plane // 2 + 1) % chips
                        pairs.append(
                            (((o * chips + z) * cores + c) * reps + r, ((o * chips + there) * cores + c) * reps + r)
                        )
        other = lax.ppermute(lax.psum(plane_sum, "core"), ALL, pairs)
    other, later = lax.optimization_barrier((other, later))
    with jax.named_scope("z_sum"):
        sums = lax.all_to_all(jnp.broadcast_to(other[None], (plane, 8, TILE)), PLANE, 0, 0, tiled=True)
    with jax.named_scope("apply"):
        return pl.pallas_call(
            functools.partial(apply_kernel, limit, count),
            out_shape=jax.ShapeDtypeStruct(resident.shape, resident.dtype),
            in_specs=[smem, vmem, vmem, vmem, hbm],
            out_specs=hbm,
            scratch_shapes=[
                pltpu.VMEM(resident.shape, resident.dtype),
                pltpu.SemaphoreType.DMA((shards,)),
                pltpu.SemaphoreType.DMA((shards,)),
            ],
            compiler_params=large,
        )(table, sums, first, later, resident)


def solution(mesh):
    outers, tensors, reps = mesh.devices.shape
    fine = Mesh(mesh.devices.reshape(outers, tensors // 2, 2, reps), ALL)
    head = ("z", "core")
    placed = (
        P(head, PEERS, None, None),
        P(head, PEERS, None, None),
        P(head, PEERS),
        P(None, head, None),
    )
    return jax.shard_map(
        body, mesh=fine, in_specs=placed, out_specs=P(None, head, None), check_vma=False
    )
```

```python
import functools
import math

import jax
import jax.numpy as jnp
from jax import lax
from jax.experimental import pallas as pl
from jax.experimental.pallas import tpu as pltpu
from jax.sharding import Mesh, PartitionSpec as P

SLOTS = 4
TILE = 128
EARLY = 64
LATER = SLOTS * TILE - EARLY
SMALL = 4 * 2**20
LARGE = 53 * 10**6
PICK = 568 * 10**5
ALL = ("outer", "z", "core", "rep")
PLANE = ("outer", "core", "rep")
PEERS = ("outer", "rep")


def pick_kernel(
    mask_hbm, master_hbm, synced_hbm, first_hbm, later_hbm, mask_ref, master_ref, synced_ref, first_ref, later_ref, sem, out_sem
):
    shards = later_hbm.shape[0]
    loads = [
        pltpu.make_async_copy(mask_hbm, mask_ref, sem.at[0]),
        pltpu.make_async_copy(master_hbm, master_ref, sem.at[1]),
        pltpu.make_async_copy(synced_hbm, synced_ref, sem.at[2]),
    ]
    for load in loads:
        load.start()
    loads[0].wait()
    where = [jnp.int32(0)] * SLOTS
    used = jnp.int32(0)
    for i in range(mask_ref.shape[1]):
        listed = mask_ref[0, i] > 0
        for s in range(SLOTS):
            where[s] = jnp.where(listed & (used == s), i, where[s])
        used = used + listed.astype(jnp.int32)
    for load in loads[1:]:
        load.wait()
    squares = jnp.zeros((8, TILE), jnp.float32)
    for s in range(SLOTS):
        delta = (master_ref[0, where[s]] - synced_ref[0, where[s]].astype(jnp.float32)).astype(jnp.bfloat16)
        if s == 0:
            first_ref[0:EARLY] = delta[0:EARLY]
            later_ref[LATER - TILE + EARLY:LATER] = delta[EARLY:TILE]
        else:
            later_ref[(s - 1) * TILE:s * TILE] = delta
        wide = jnp.where(used > s, delta.astype(jnp.float32), 0.0)
        squares = squares + jnp.sum((wide * wide).reshape(-1, 8, TILE), axis=0)
    sends = [pltpu.make_async_copy(later_ref, later_hbm.at[j], out_sem.at[0, j]) for j in range(shards)]
    for send in sends:
        send.start()
    lane = lax.broadcasted_iota(jnp.int32, (16, TILE), 1)
    total = jnp.full((16, TILE), jnp.sum(squares), jnp.float32)
    high = total.astype(jnp.bfloat16).astype(jnp.float32)
    middle = (total - high).astype(jnp.bfloat16).astype(jnp.float32)
    low = total - high - middle
    note = jnp.where(lane == 0, high, jnp.where(lane == 8, middle, jnp.where(lane == 9, low, 0.0)))
    for k, entry in enumerate([used] + where):
        note = jnp.where(lane == 1 + k, entry.astype(jnp.float32), note)
    first_ref[EARLY:EARLY + 16] = note.astype(jnp.bfloat16)
    firsts = [pltpu.make_async_copy(first_ref, first_hbm.at[j], out_sem.at[1, j]) for j in range(shards)]
    for send in firsts:
        send.start()
    for send in sends + firsts:
        send.wait()


def plane_kernel(first_ref, sum_ref, table_ref):
    shards = first_ref.shape[0]
    lane = lax.broadcasted_iota(jnp.int32, (16, TILE), 1)
    part = (lane == 0) | (lane == 8) | (lane == 9)
    total = jnp.zeros((16, TILE), jnp.float32)
    for j in range(shards):
        note = first_ref[j, EARLY:EARLY + 16].astype(jnp.float32)
        total = total + jnp.sum(jnp.where(part, note, 0.0), axis=1, keepdims=True)
        table_ref[j:j + 1, :] = jnp.where(part, 0.0, note)[0:1].astype(jnp.int32)
    sum_ref[...] = total[0:8]


def apply_kernel(
    limit, count, table_ref, sums_ref, first_ref, later_ref, resident_hbm, out_hbm, rows_ref, in_sem, out_sem
):
    shards = table_ref.shape[0]
    wide = count * TILE
    per_layer = resident_hbm.shape[2] // wide

    def block(ref, j):
        return ref.at[j // per_layer, :, pl.ds((j % per_layer) * wide, wide)]

    loads = [pltpu.make_async_copy(block(resident_hbm, j), block(rows_ref, j), in_sem.at[j]) for j in range(shards)]
    stores = [pltpu.make_async_copy(block(rows_ref, j), block(out_hbm, j), out_sem.at[j]) for j in range(shards)]
    for load in loads:
        load.start()
    total = jnp.sum(sums_ref[...], axis=0)
    factor = jnp.minimum(jnp.float32(1.0), limit / jnp.sqrt(total))[None]
    for j in range(shards):
        loads[j].wait()

        def add(slot, tile):
            start = pl.multiple_of((j % per_layer) * wide + table_ref[j, 2 + slot] * TILE, TILE)
            place = (j // per_layer, slice(None), pl.ds(start, TILE))
            moved = (factor * tile.astype(jnp.float32).reshape(-1, 8, TILE)).reshape(TILE, TILE)
            rows_ref[place] = (rows_ref[place].astype(jnp.float32) + moved).astype(jnp.bfloat16)

        @pl.when(table_ref[j, 1] > 0)
        def _():
            rest = later_ref[j, LATER - TILE + EARLY:LATER]
            add(0, jnp.concatenate([first_ref[j, 0:EARLY], rest], axis=0))

        def later(s, _):
            add(s, later_ref[j, pl.ds(pl.multiple_of((s - 1) * TILE, TILE), TILE)])
            return 0

        lax.fori_loop(1, table_ref[j, 1], later, 0)
        stores[j].start()
    for store in stores:
        store.wait()


def body(master, synced, keep_mask, resident):
    outers, chips, cores, reps = (lax.axis_size(a) for a in ALL)
    _, count, side, _ = master.shape
    shards = outers * reps
    plane = shards * cores
    limit = 0.25 * side * math.sqrt(count * plane * plane)
    vmem = pl.BlockSpec(memory_space=pltpu.VMEM)
    smem = pl.BlockSpec(memory_space=pltpu.SMEM)
    hbm = pl.BlockSpec(memory_space=pl.ANY)
    small = pltpu.CompilerParams(vmem_limit_bytes=SMALL)
    large = pltpu.CompilerParams(vmem_limit_bytes=LARGE)
    with jax.named_scope("pick"):
        first, later = pl.pallas_call(
            pick_kernel,
            out_shape=(
                jax.ShapeDtypeStruct((shards, EARLY + 16, side), jnp.bfloat16),
                jax.ShapeDtypeStruct((shards, LATER, side), jnp.bfloat16),
            ),
            in_specs=[hbm, hbm, hbm],
            out_specs=(hbm, hbm),
            scratch_shapes=[
                pltpu.SMEM(keep_mask.shape, keep_mask.dtype),
                pltpu.VMEM(master.shape, master.dtype),
                pltpu.VMEM(synced.shape, synced.dtype),
                pltpu.VMEM((EARLY + 16, side), jnp.bfloat16),
                pltpu.VMEM((LATER, side), jnp.bfloat16),
                pltpu.SemaphoreType.DMA((3,)),
                pltpu.SemaphoreType.DMA((2, shards)),
            ],
        )(keep_mask, master, synced)
    with jax.named_scope("first_slot"):
        first = lax.all_to_all(first, PEERS, 0, 0, tiled=True)
        plane_sum, table = pl.pallas_call(
            plane_kernel,
            out_shape=(
                jax.ShapeDtypeStruct((8, TILE), jnp.float32),
                jax.ShapeDtypeStruct((shards, TILE), jnp.int32),
            ),
            in_specs=[vmem],
            out_specs=(vmem, vmem),
            compiler_params=small,
        )(first)
    later, plane_sum = lax.optimization_barrier((later, plane_sum))
    with jax.named_scope("later_slots"):
        later = lax.all_to_all(later, PEERS, 0, 0, tiled=True)
    with jax.named_scope("z_shift"):
        pairs = []
        for o in range(outers):
            for z in range(chips):
                for c in range(cores):
                    for r in range(reps):
                        there = (z + (o * cores + c) * reps + r - plane // 2 + 1) % chips
                        pairs.append(
                            (((o * chips + z) * cores + c) * reps + r, ((o * chips + there) * cores + c) * reps + r)
                        )
        other = lax.ppermute(lax.psum(plane_sum, "core"), ALL, pairs)
    other, later = lax.optimization_barrier((other, later))
    with jax.named_scope("z_sum"):
        sums = lax.all_to_all(jnp.broadcast_to(other[None], (plane, 8, TILE)), PLANE, 0, 0, tiled=True)
    with jax.named_scope("apply"):
        return pl.pallas_call(
            functools.partial(apply_kernel, limit, count),
            out_shape=jax.ShapeDtypeStruct(resident.shape, resident.dtype),
            in_specs=[smem, vmem, vmem, vmem, hbm],
            out_specs=hbm,
            scratch_shapes=[
                pltpu.VMEM(resident.shape, resident.dtype),
                pltpu.SemaphoreType.DMA((shards,)),
                pltpu.SemaphoreType.DMA((shards,)),
            ],
            compiler_params=large,
        )(table, sums, first, later, resident)


def solution(mesh):
    outers, tensors, reps = mesh.devices.shape
    fine = Mesh(mesh.devices.reshape(outers, tensors // 2, 2, reps), ALL)
    head = ("z", "core")
    placed = (
        P(head, PEERS, None, None),
        P(head, PEERS, None, None),
        P(head, PEERS),
        P(None, head, None),
    )
    return jax.shard_map(
        body, mesh=fine, in_specs=placed, out_specs=P(None, head, None), check_vma=False
    )
```

```python
import functools
import math

import jax
import jax.numpy as jnp
from jax import lax
from jax.experimental import pallas as pl
from jax.experimental.pallas import tpu as pltpu
from jax.sharding import Mesh, PartitionSpec as P

SLOTS = 4
LATER = SLOTS - 1
TILE = 128
SMALL = 4 * 2**20
LARGE = 53 * 10**6
PICK = 568 * 10**5
ALL = ("outer", "z", "core", "rep")
PLANE = ("outer", "core", "rep")
PEERS = ("outer", "rep")


def pick_kernel(
    mask_hbm, master_hbm, synced_hbm, first_hbm, later_hbm, mask_ref, master_ref, synced_ref, first_ref, later_ref, sem, out_sem
):
    shards = later_hbm.shape[0]
    loads = [
        pltpu.make_async_copy(mask_hbm, mask_ref, sem.at[0]),
        pltpu.make_async_copy(master_hbm, master_ref, sem.at[1]),
        pltpu.make_async_copy(synced_hbm, synced_ref, sem.at[2]),
    ]
    for load in loads:
        load.start()
    loads[0].wait()
    where = [jnp.int32(0)] * SLOTS
    used = jnp.int32(0)
    for i in range(mask_ref.shape[1]):
        listed = mask_ref[0, i] > 0
        for s in range(SLOTS):
            where[s] = jnp.where(listed & (used == s), i, where[s])
        used = used + listed.astype(jnp.int32)
    for load in loads[1:]:
        load.wait()
    squares = jnp.zeros((8, TILE), jnp.float32)
    for s in range(SLOTS):
        delta = (master_ref[0, where[s]] - synced_ref[0, where[s]].astype(jnp.float32)).astype(jnp.bfloat16)
        if s == 0:
            first_ref[0:TILE] = delta
        else:
            later_ref[s - 1] = delta
        wide = jnp.where(used > s, delta.astype(jnp.float32), 0.0)
        squares = squares + jnp.sum((wide * wide).reshape(-1, 8, TILE), axis=0)
    sends = [pltpu.make_async_copy(later_ref, later_hbm.at[j], out_sem.at[0, j]) for j in range(shards)]
    for send in sends:
        send.start()
    lane = lax.broadcasted_iota(jnp.int32, (16, TILE), 1)
    total = jnp.full((16, TILE), jnp.sum(squares), jnp.float32)
    high = total.astype(jnp.bfloat16).astype(jnp.float32)
    middle = (total - high).astype(jnp.bfloat16).astype(jnp.float32)
    low = total - high - middle
    note = jnp.where(lane == 0, high, jnp.where(lane == 8, middle, jnp.where(lane == 9, low, 0.0)))
    for k, entry in enumerate([used] + where):
        note = jnp.where(lane == 1 + k, entry.astype(jnp.float32), note)
    first_ref[TILE:TILE + 16] = note.astype(jnp.bfloat16)
    firsts = [pltpu.make_async_copy(first_ref, first_hbm.at[j], out_sem.at[1, j]) for j in range(shards)]
    for send in firsts:
        send.start()
    for send in sends + firsts:
        send.wait()


def plane_kernel(first_ref, sum_ref, table_ref):
    shards = first_ref.shape[0]
    lane = lax.broadcasted_iota(jnp.int32, (16, TILE), 1)
    part = (lane == 0) | (lane == 8) | (lane == 9)
    total = jnp.zeros((16, TILE), jnp.float32)
    for j in range(shards):
        note = first_ref[j, TILE:TILE + 16].astype(jnp.float32)
        total = total + jnp.sum(jnp.where(part, note, 0.0), axis=1, keepdims=True)
        table_ref[j:j + 1, :] = jnp.where(part, 0.0, note)[0:1].astype(jnp.int32)
    sum_ref[...] = total[0:8]


def apply_kernel(
    limit, count, table_ref, sums_ref, first_ref, later_ref, resident_hbm, out_hbm, rows_ref, in_sem, out_sem
):
    shards = table_ref.shape[0]
    wide = count * TILE
    per_layer = resident_hbm.shape[2] // wide

    def block(ref, j):
        return ref.at[j // per_layer, :, pl.ds((j % per_layer) * wide, wide)]

    loads = [pltpu.make_async_copy(block(resident_hbm, j), block(rows_ref, j), in_sem.at[j]) for j in range(shards)]
    stores = [pltpu.make_async_copy(block(rows_ref, j), block(out_hbm, j), out_sem.at[j]) for j in range(shards)]
    for load in loads:
        load.start()
    total = jnp.sum(sums_ref[...], axis=0)
    factor = jnp.minimum(jnp.float32(1.0), limit / jnp.sqrt(total))[None]
    for j in range(shards):
        loads[j].wait()

        def add(slot, tile):
            start = pl.multiple_of((j % per_layer) * wide + table_ref[j, 2 + slot] * TILE, TILE)
            place = (j // per_layer, slice(None), pl.ds(start, TILE))
            moved = (factor * tile.astype(jnp.float32).reshape(-1, 8, TILE)).reshape(TILE, TILE)
            rows_ref[place] = (rows_ref[place].astype(jnp.float32) + moved).astype(jnp.bfloat16)

        @pl.when(table_ref[j, 1] > 0)
        def _():
            add(0, first_ref[j, 0:TILE])

        def later(s, _):
            add(s, later_ref[j * LATER + s - 1])
            return 0

        lax.fori_loop(1, table_ref[j, 1], later, 0)
        stores[j].start()
    for store in stores:
        store.wait()


def body(master, synced, keep_mask, resident):
    outers, chips, cores, reps = (lax.axis_size(a) for a in ALL)
    _, count, side, _ = master.shape
    shards = outers * reps
    plane = shards * cores
    limit = 0.25 * side * math.sqrt(count * plane * plane)
    vmem = pl.BlockSpec(memory_space=pltpu.VMEM)
    smem = pl.BlockSpec(memory_space=pltpu.SMEM)
    hbm = pl.BlockSpec(memory_space=pl.ANY)
    small = pltpu.CompilerParams(vmem_limit_bytes=SMALL)
    large = pltpu.CompilerParams(vmem_limit_bytes=LARGE)
    with jax.named_scope("pick"):
        first, later = pl.pallas_call(
            pick_kernel,
            out_shape=(
                jax.ShapeDtypeStruct((shards, side + 16, side), jnp.bfloat16),
                jax.ShapeDtypeStruct((shards, LATER, side, side), jnp.bfloat16),
            ),
            in_specs=[hbm, hbm, hbm],
            out_specs=(hbm, hbm),
            scratch_shapes=[
                pltpu.SMEM(keep_mask.shape, keep_mask.dtype),
                pltpu.VMEM(master.shape, master.dtype),
                pltpu.VMEM(synced.shape, synced.dtype),
                pltpu.VMEM((side + 16, side), jnp.bfloat16),
                pltpu.VMEM((LATER, side, side), jnp.bfloat16),
                pltpu.SemaphoreType.DMA((3,)),
                pltpu.SemaphoreType.DMA((2, shards)),
            ],
        )(keep_mask, master, synced)
    with jax.named_scope("first_slot"):
        first = lax.all_to_all(first, PEERS, 0, 0, tiled=True)
        plane_sum, table = pl.pallas_call(
            plane_kernel,
            out_shape=(
                jax.ShapeDtypeStruct((8, TILE), jnp.float32),
                jax.ShapeDtypeStruct((shards, TILE), jnp.int32),
            ),
            in_specs=[vmem],
            out_specs=(vmem, vmem),
            compiler_params=small,
        )(first)
        plane_sum = lax.psum(plane_sum, "core")
    later, plane_sum = lax.optimization_barrier((later, plane_sum))
    with jax.named_scope("later_slots"):
        later = lax.all_to_all(later, PEERS, 0, 0, tiled=True)
        later = later.reshape(shards * LATER, side, side)
    with jax.named_scope("z_shift"):
        pairs = []
        for o in range(outers):
            for z in range(chips):
                for c in range(cores):
                    for r in range(reps):
                        there = (z + (o * cores + c) * reps + r - plane // 2 + 1) % chips
                        pairs.append(
                            (((o * chips + z) * cores + c) * reps + r, ((o * chips + there) * cores + c) * reps + r)
                        )
        other = lax.ppermute(plane_sum, ALL, pairs)
    other, later = lax.optimization_barrier((other, later))
    with jax.named_scope("z_sum"):
        sums = lax.all_to_all(jnp.broadcast_to(other[None], (plane, 8, TILE)), PLANE, 0, 0, tiled=True)
    with jax.named_scope("apply"):
        return pl.pallas_call(
            functools.partial(apply_kernel, limit, count),
            out_shape=jax.ShapeDtypeStruct(resident.shape, resident.dtype),
            in_specs=[smem, vmem, vmem, vmem, hbm],
            out_specs=hbm,
            scratch_shapes=[
                pltpu.VMEM(resident.shape, resident.dtype),
                pltpu.SemaphoreType.DMA((shards,)),
                pltpu.SemaphoreType.DMA((shards,)),
            ],
            compiler_params=large,
        )(table, sums, first, later, resident)


def solution(mesh):
    outers, tensors, reps = mesh.devices.shape
    fine = Mesh(mesh.devices.reshape(outers, tensors // 2, 2, reps), ALL)
    head = ("z", "core")
    placed = (
        P(head, PEERS, None, None),
        P(head, PEERS, None, None),
        P(head, PEERS),
        P(None, head, None),
    )
    return jax.shard_map(
        body, mesh=fine, in_specs=placed, out_specs=P(None, head, None), check_vma=False
    )
```
